32 devices in a mesh: energy: 8 (over y, x, core), slab: 4 (over z).
Axes of the slice: x: 2, y: 2, z: 4, core: 2. Of those that a mesh axis runs over, the one named last changes fastest.
Arguments:
- g_lesser: bfloat16 [8, 4, 320, 640], P('energy', 'slab'), may hold values from -6 to 6
- g_retarded: bfloat16 [8, 4, 320, 640], P('energy', 'slab'), may hold values from -0.25 to 0.25
- screened: bfloat16 [8, 4, 320, 640], P(None, 'slab', 'energy'), may hold values from -2 to 2
- coupling: bfloat16 [4, 320, 320], P('slab'), may hold values from -1.5 to 1.5, as said below
Outputs:
- correction: bfloat16 [8, 4, 320, 640], P('energy', 'slab')
The draws below stay inside these ranges and needn't reach their ends.
Inputs may be any that keep to these rules, and one draw needn't show every extreme that they name: `coupling`: coupling_s is the diagonal entries between 0.75 and 1 plus independent small entries.
All inputs are finite; a program needn't handle non-finite values.
Results may differ from the reference program's by a relative error of at most 0.02.
Values may be sent and summed in bfloat16 or wider, within the bound.
No kernel may reach another device: no remote copies, remote signals or barrier semaphores. Data moves between devices by JAX's collectives and lax.ppermute only.
A program may use at most 64 MiB of HBM per device.

```python
import jax
import jax.numpy as jnp
from jax import lax

B = 320
NE = 8
SLABS = 4


def draw_coupling(key, part):
    first = jax.random.fold_in(key, 11)
    second = jax.random.fold_in(key, 12)
    diagonal = jax.random.uniform(first, (SLABS, B), jnp.float32, 0.75, 1.0)
    spread = jnp.clip(jax.random.normal(second, (SLABS, B, B), jnp.float32), -4.0, 4.0) * (0.3 / jnp.sqrt(jnp.float32(B)))
    matrix = spread + jnp.eye(B, dtype=jnp.float32)[None] * diagonal[:, :, None]
    return matrix.astype(jnp.bfloat16)


def block_levels(own_key, extent, cuts, least, top_value):
    def one(axis_at, blocks):
        heights = jax.random.uniform(jax.random.fold_in(jax.random.fold_in(own_key, 6), axis_at), (blocks,), jnp.float32, least / len(cuts), top_value / len(cuts))
        return jnp.repeat(jnp.exp(heights), extent[axis_at] // blocks).reshape((-1,) + (1,) * (len(extent) - axis_at - 1))

    loudness = one(*cuts[0])
    for cut in cuts[1:]:
        loudness = loudness * one(*cut)
    return loudness


def gaussian(key, dims, scale, reach, split=(), kind=jnp.bfloat16):
    factor_of = block_levels(key, dims, split, -0.22, 0.18) if split else 1.0
    array = jax.random.normal(key, dims, jnp.float32) * scale * factor_of
    return jnp.minimum(jnp.maximum(array, -reach), reach).astype(kind)


def setup_inputs(seed: int = 0) -> dict:
    key_of = jax.random.split(jax.random.key(seed), 5)
    return {
        "g_lesser": gaussian(key_of[0], (NE, SLABS, B, 2 * B), 1.0, 6.0, ((0, 8), (1, 4))),
        "g_retarded": gaussian(key_of[1], (NE, SLABS, B, 2 * B), (2 * B) ** -0.5, 0.25, ((0, 8), (1, 4))),
        "screened": gaussian(key_of[2], (NE, SLABS, B, 2 * B), NE ** -0.5, 2.0, ((1, 4), (2, 8))),
        "coupling": draw_coupling(jax.random.fold_in(key_of[4], 71), 0),
    }


def convolve(lesser, screened):
    half = lesser.shape[-1] // 2
    count = lesser.shape[0]
    grid = lesser.astype(jnp.float32)
    inter = screened.astype(jnp.float32)
    lesser_c = grid[..., :half] + 1j * grid[..., half:]
    inter_c = inter[..., :half] + 1j * inter[..., half:]
    length = 2 * count
    product = jnp.fft.fft(lesser_c, n=length, axis=0) * jnp.fft.fft(inter_c, n=length, axis=0)
    conv = jnp.fft.ifft(product, axis=0)[:count]
    return jnp.concatenate([-conv.imag, conv.real], axis=-1).astype(jnp.bfloat16)


def transport(coupling, state):
    count = state.shape[0]
    half = state.shape[-1] // 2
    left = jnp.einsum("ab,nbc->nac", coupling.astype(jnp.float32), state.astype(jnp.float32)).astype(jnp.bfloat16)
    parts = left.reshape(count, half, 2, half)
    moved = jnp.einsum("nakb,cb->nakc", parts.astype(jnp.float32), coupling.astype(jnp.float32))
    return moved.reshape(count, half, 2 * half)


def sandwich(green, state):
    half = green.shape[-1] // 2
    green_re = green[..., :half]
    green_im = green[..., half:]
    state_re = state[..., :half]
    state_im = state[..., half:]
    right_mat = jnp.concatenate([jnp.concatenate([state_re, state_im], -1), jnp.concatenate([-state_im, state_re], -1)], 1)
    left = jnp.einsum("nab,nbc->nac", green.astype(jnp.float32), right_mat.astype(jnp.float32)).astype(jnp.bfloat16)
    tr_re = jnp.swapaxes(green_re, 1, 2)
    tr_im = jnp.swapaxes(green_im, 1, 2)
    adjoint = jnp.concatenate([jnp.concatenate([tr_re, -tr_im], -1), jnp.concatenate([tr_im, tr_re], -1)], 1)
    return jnp.einsum("nab,nbc->nac", left.astype(jnp.float32), adjoint.astype(jnp.float32)).astype(jnp.bfloat16)


def reference(g_lesser, g_retarded, screened, coupling):
    def slab_step(state, index):
        lesser = lax.dynamic_index_in_dim(g_lesser, index, 1, keepdims=False)
        inter = lax.dynamic_index_in_dim(screened, index, 1, keepdims=False)
        green = lax.dynamic_index_in_dim(g_retarded, index, 1, keepdims=False)
        link = lax.dynamic_index_in_dim(coupling, index, 0, keepdims=False)
        sigma = convolve(lesser, inter)
        fresh = sigma.astype(jnp.float32) + transport(link, state.astype(jnp.bfloat16))
        return fresh, sandwich(green, fresh.astype(jnp.bfloat16))

    start = jnp.zeros((NE, B, 2 * B), jnp.float32)
    final, blocks = lax.scan(slab_step, start, jnp.arange(SLABS, dtype=jnp.int32))
    return jnp.swapaxes(blocks, 0, 1)
```

```python
import functools

import jax
import jax.numpy as jnp
from jax import lax
from jax.experimental import pallas as pl
from jax.experimental.pallas import tpu as pltpu
from jax.sharding import PartitionSpec as P

ENERGY = "energy"
SLAB = "slab"
WHOLE = pl.BlockSpec(memory_space=pltpu.VMEM)
SCALAR = pl.BlockSpec(memory_space=pltpu.SMEM)


def in_vmem(*arrays):
    return [pltpu.with_memory_space_constraint(x, pltpu.VMEM) for x in arrays]


def swap_with(array, mask):
    devices = lax.axis_size(ENERGY)
    return lax.ppermute(array, ENERGY, [(i, i ^ mask) for i in range(devices)])


def conv_kernel(chips, place_ref, inter_ref, *refs):
    pieces = refs[: 2 * chips]
    re_ref, im_ref, a_ref, b_ref, w_ref, v_ref, sum_ref = refs[2 * chips :]
    chip, side = place_ref[0], place_ref[1]
    rows, width = inter_ref.shape[1:]
    half = width // 2
    left = lax.broadcasted_iota(jnp.int32, (rows, width), 1) < half

    def swapped(x):
        return jnp.concatenate([x[:, half:], x[:, :half]], axis=1)

    @pl.when(side == 0)
    def _():
        a_ref[0] = jnp.zeros((rows, width), jnp.float32)
        b_ref[0] = jnp.zeros((rows, width), jnp.float32)

    for other in range(2):
        for j in range(chips):
            x = pieces[other * chips + j][...].astype(jnp.float32)
            y = swapped(x)
            slot = 2 * (chip ^ j) + (side ^ other) + 1 - side
            a_ref[slot] = jnp.where(left, x, y)
            b_ref[slot] = jnp.where(left, y, x)
    for m in range(2 * chips):
        x = inter_ref[m].astype(jnp.float32)
        y = swapped(x)
        w_ref[m] = x
        v_ref[m] = jnp.where(left, -y, y)

    step = 8 if rows % 8 == 0 else rows
    lanes = 128 if width % 128 == 0 else width

    def tile(t, carry):
        here = pl.ds(pl.multiple_of(t * step, step), step)
        for c in range(0, width, lanes):
            at = pl.ds(c, lanes)
            for j in range(chips):
                total = None
                for m in range(2 * j + 2):
                    s = 2 * j + 1 - m
                    term = a_ref[s, here, at] * v_ref[m, here, at] - b_ref[s, here, at] * w_ref[m, here, at]
                    total = term if total is None else total + term
                sum_ref[j, here, at] = total
        return carry

    lax.fori_loop(0, rows // step, tile, 0)
    for j in range(chips):
        out = sum_ref[j].astype(jnp.bfloat16)
        re_ref[chip ^ j] = out[:, :half]
        im_ref[chip ^ j] = out[:, half:]


def convolve(chips, place, inter, pieces):
    count, rows, width = inter.shape
    part = pltpu.VMEM((chips, rows, width // 2), jnp.bfloat16)
    block = lambda n: pltpu.VMEM((n, rows, width), jnp.float32)
    return pl.pallas_call(
        functools.partial(conv_kernel, chips),
        out_shape=[part, part],
        in_specs=[SCALAR] + [WHOLE] * (1 + 2 * chips),
        out_specs=[WHOLE, WHOLE],
        scratch_shapes=[block(count + 1), block(count + 1), block(count), block(count), block(chips)],
        compiler_params=pltpu.CompilerParams(vmem_limit_bytes=24 << 20),
        cost_estimate=pl.CostEstimate(flops=count * count * rows * width * 4, bytes_accessed=0, transcendentals=0),
    )(place, *in_vmem(inter, *pieces))


def gather_kernel(place_ref, first_ref, *refs):
    chip = place_ref[0]
    out_ref = refs[-1]
    out_ref[chip] = first_ref[0]
    for j, ref in enumerate(refs[:-1]):
        out_ref[chip ^ (j + 1)] = ref[...]


def gathered(place, own, pieces):
    chips, rows, half = own.shape
    out = pl.pallas_call(
        gather_kernel,
        out_shape=pltpu.VMEM((chips, rows, half), jnp.bfloat16),
        in_specs=[SCALAR] + [WHOLE] * chips,
        out_specs=WHOLE,
    )(place, *in_vmem(own, *pieces))
    return out.reshape(chips * rows, half)


def moved(link, state):
    left = jnp.dot(link, state, preferred_element_type=jnp.float32).astype(jnp.bfloat16)
    return lax.dot_general(left, link, (((1,), (1,)), ((), ())), preferred_element_type=jnp.float32)


def sandwich(green, state_re, state_im):
    half = green.shape[-1] // 2
    green_re, green_im = green[:, :half], green[:, half:]

    def dot(a, b):
        return jnp.dot(a, b, preferred_element_type=jnp.float32)

    def dot_t(a, b):
        return lax.dot_general(a, b, (((1,), (1,)), ((), ())), preferred_element_type=jnp.float32)

    left_re = (dot(green_re, state_re) - dot(green_im, state_im)).astype(jnp.bfloat16)
    left_im = (dot(green_re, state_im) + dot(green_im, state_re)).astype(jnp.bfloat16)
    out_re = dot_t(left_re, green_re) + dot_t(left_im, green_im)
    out_im = dot_t(left_im, green_re) - dot_t(left_re, green_im)
    return jnp.concatenate([out_re, out_im], axis=-1).astype(jnp.bfloat16)


def local(g_lesser, g_retarded, screened, coupling):
    devices = lax.axis_size(ENERGY)
    slabs = lax.axis_size(SLAB)
    chips = devices // 2
    me = lax.axis_index(ENERGY)
    slab = lax.axis_index(SLAB)
    chip, side = me // 2, me % 2
    place = jnp.stack([chip, side]).astype(jnp.int32)

    lesser = g_lesser[0, 0]
    size, width = lesser.shape
    rows = size // chips
    inter = screened[:, 0]
    inter_other = swap_with(inter, 1)
    first = jnp.where(side == 0, inter, inter_other)
    second = jnp.where(side == 0, inter_other, inter)
    inter_rows = jnp.concatenate([first, second], axis=1)

    mine = [lax.dynamic_slice(lesser, (rows * (chip ^ j), 0), (rows, width)) for j in range(chips)]
    pieces = [mine[0]] + [swap_with(mine[j], 2 * j) for j in range(1, chips)]
    pieces = pieces + [swap_with(x, 1) for x in pieces]
    re_rows, im_rows = convolve(chips, place, inter_rows, pieces)

    re_parts = [swap_with(re_rows[j], 2 * j) for j in range(1, chips)]
    im_parts = [swap_with(im_rows[j], 2 * j) for j in range(1, chips)]
    sigma_re = gathered(place, re_rows, re_parts)
    sigma_im = gathered(place, im_rows, im_parts)

    link = coupling[0]
    payload = sigma_re
    state_re = sigma_re
    for p in range(1, slabs + 1):
        pairs = [(s, s + 1) for s in (p - 1, p - 2) if 0 <= s and s + 1 < slabs]
        came = lax.ppermute(payload, SLAB, pairs)
        base = jnp.where(slab >= p, sigma_re, sigma_im)
        payload = (base.astype(jnp.float32) + moved(link, came)).astype(jnp.bfloat16)
        state_re = jnp.where(slab == p, payload, state_re)
        state_im = payload if p == 1 else jnp.where(slab + 1 == p, payload, state_im)
    return sandwich(g_retarded[0, 0], state_re, state_im)[None, None]


def solution(mesh):
    placed = (
        P(ENERGY, SLAB, None, None),
        P(ENERGY, SLAB, None, None),
        P(None, SLAB, ENERGY, None),
        P(SLAB, None, None),
    )
    return jax.shard_map(
        local,
        mesh=mesh,
        in_specs=placed,
        out_specs=P(ENERGY, SLAB, None, None),
        check_vma=False,
    )
```

```python
import functools

import jax
import jax.numpy as jnp
from jax import lax
from jax.experimental import pallas as pl
from jax.experimental.pallas import tpu as pltpu
from jax.sharding import PartitionSpec as P

ENERGY = "energy"
SLAB = "slab"
WHOLE = pl.BlockSpec(memory_space=pltpu.VMEM)
SCALAR = pl.BlockSpec(memory_space=pltpu.SMEM)


def in_vmem(*arrays):
    return [pltpu.with_memory_space_constraint(x, pltpu.VMEM) for x in arrays]


def swap_with(array, mask):
    devices = lax.axis_size(ENERGY)
    return lax.ppermute(array, ENERGY, [(i, i ^ mask) for i in range(devices)])


def swap_across(array, mask):
    devices, slabs = lax.axis_size(ENERGY), lax.axis_size(SLAB)
    pairs = [(e * slabs + s, (e ^ mask) * slabs + (s ^ 1)) for e in range(devices) for s in range(slabs)]
    return lax.ppermute(array, (ENERGY, SLAB), pairs)


def conv_kernel(chips, place_ref, inter_ref, *refs):
    pieces = refs[: 2 * chips]
    out_ref, a_ref, b_ref, w_ref, v_ref, sum_ref = refs[2 * chips :]
    chip, side = place_ref[0], place_ref[1]
    rows, width = inter_ref.shape[1:]
    half = width // 2
    left = lax.broadcasted_iota(jnp.int32, (rows, width), 1) < half

    def swapped(x):
        return jnp.concatenate([x[:, half:], x[:, :half]], axis=1)

    @pl.when(side == 0)
    def _():
        a_ref[0] = jnp.zeros((rows, width), jnp.float32)
        b_ref[0] = jnp.zeros((rows, width), jnp.float32)

    for other in range(2):
        for j in range(chips):
            x = pieces[other * chips + j][...].astype(jnp.float32)
            y = swapped(x)
            slot = 2 * (chip ^ j) + (side ^ other) + 1 - side
            a_ref[slot] = jnp.where(left, x, y)
            b_ref[slot] = jnp.where(left, y, x)
    for m in range(2 * chips):
        x = inter_ref[m].astype(jnp.float32)
        y = swapped(x)
        w_ref[m] = x
        v_ref[m] = jnp.where(left, -y, y)

    step = 8 if rows % 8 == 0 else rows
    lanes = 128 if width % 128 == 0 else width

    def tile(t, carry):
        here = pl.ds(pl.multiple_of(t * step, step), step)
        for c in range(0, width, lanes):
            at = pl.ds(c, lanes)
            for j in range(chips):
                total = None
                for m in range(2 * j + 2):
                    s = 2 * j + 1 - m
                    term = a_ref[s, here, at] * v_ref[m, here, at] - b_ref[s, here, at] * w_ref[m, here, at]
                    total = term if total is None else total + term
                sum_ref[chip ^ j, here, at] = total
        return carry

    lax.fori_loop(0, rows // step, tile, 0)
    out_ref[...] = sum_ref[...].astype(jnp.bfloat16)


def convolve(chips, place, inter, pieces):
    count, rows, width = inter.shape
    block = lambda n: pltpu.VMEM((n, rows, width), jnp.float32)
    return pl.pallas_call(
        functools.partial(conv_kernel, chips),
        out_shape=pltpu.VMEM((chips, rows, width), jnp.bfloat16),
        in_specs=[SCALAR] + [WHOLE] * (1 + 2 * chips),
        out_specs=WHOLE,
        scratch_shapes=[block(count + 1), block(count + 1), block(count), block(count), block(chips)],
        compiler_params=pltpu.CompilerParams(vmem_limit_bytes=24 << 20),
        cost_estimate=pl.CostEstimate(flops=count * count * rows * width * 4, bytes_accessed=0, transcendentals=0),
    )(place, *in_vmem(inter, *pieces))


def dot(a, b):
    return jnp.dot(a, b, preferred_element_type=jnp.float32)


def dot_t(a, b):
    return lax.dot_general(a, b, (((1,), (1,)), ((), ())), preferred_element_type=jnp.float32)


def moved(link, parts):
    size = link.shape[0]
    left = jnp.concatenate([dot(link, x).astype(jnp.bfloat16) for x in parts], axis=0)
    out = dot_t(left, link)
    return [out[i * size : (i + 1) * size] for i in range(len(parts))]


def first_kernel(chips, place_ref, link_ref, *refs):
    own, before = refs[:chips], refs[chips : 2 * chips]
    re_ref, im_ref, own_ref, before_ref = refs[2 * chips :]
    chip, odd = place_ref[0], place_ref[2]
    for j in range(chips):
        own_ref[chip ^ j] = own[j][...]
        before_ref[chip ^ j] = before[j][...]
    _, rows, width = own_ref.shape
    half = width // 2
    x = own_ref[...].reshape(chips * rows, width)

    @pl.when(odd == 0)
    def _():
        re_ref[...] = x[:, :half]
        im_ref[...] = x[:, half:]

    @pl.when(odd == 1)
    def _():
        y = before_ref[...].reshape(chips * rows, width)
        re, im = moved(link_ref[...], [y[:, :half], y[:, half:]])
        re_ref[...] = (x[:, :half].astype(jnp.float32) + re).astype(jnp.bfloat16)
        im_ref[...] = (x[:, half:].astype(jnp.float32) + im).astype(jnp.bfloat16)


def first_state(chips, place, link, own, before):
    rows, width = own[0].shape
    part = pltpu.VMEM((chips * rows, width // 2), jnp.bfloat16)
    block = pltpu.VMEM((chips, rows, width), jnp.bfloat16)
    return pl.pallas_call(
        functools.partial(first_kernel, chips),
        out_shape=[part, part],
        in_specs=[SCALAR] + [WHOLE] * (1 + 2 * chips),
        out_specs=[WHOLE, WHOLE],
        scratch_shapes=[block, block],
    )(place, *in_vmem(link, *own, *before))


def advance(place_ref, link_ref, link_before_ref, re_ref, im_ref, early_im_ref, early_re_ref, late_ref, x_ref):
    odd = place_ref[2]

    @pl.when(odd == 0)
    def _():
        x_ref[0] = late_ref[...]
        x_ref[1] = early_im_ref[...]

    @pl.when(odd == 1)
    def _():
        parts = moved(link_before_ref[...], [early_re_ref[...], late_ref[...]])
        x_ref[0] = parts[0].astype(jnp.bfloat16)
        x_ref[1] = parts[1].astype(jnp.bfloat16)

    re, im = moved(link_ref[...], [x_ref[0], x_ref[1]])
    return (
        (re_ref[...].astype(jnp.float32) + re).astype(jnp.bfloat16),
        (im_ref[...].astype(jnp.float32) + im).astype(jnp.bfloat16),
    )


def advance_kernel(*refs):
    *given, new_re_ref, new_im_ref, x_ref = refs
    new_re_ref[...], new_im_ref[...] = advance(*given, x_ref)


def last_kernel(*refs):
    *given, green_ref, out_ref, x_ref = refs
    re, im = advance(*given, x_ref)
    half = re.shape[1]
    green = green_ref[...]
    green_re, green_im = green[:, :half], green[:, half:]
    right = jnp.concatenate([jnp.concatenate([re, im], axis=1), jnp.concatenate([-im, re], axis=1)], axis=0)
    left = dot(green, right).astype(jnp.bfloat16)
    adjoint = jnp.concatenate([green, jnp.concatenate([-green_im, green_re], axis=1)], axis=0)
    out_ref[...] = dot_t(left, adjoint).astype(jnp.bfloat16)


def next_state(*given):
    part = pltpu.VMEM(given[3].shape, jnp.bfloat16)
    return pl.pallas_call(
        advance_kernel,
        out_shape=[part, part],
        in_specs=[SCALAR] + [WHOLE] * (len(given) - 1),
        out_specs=[WHOLE, WHOLE],
        scratch_shapes=[pltpu.VMEM((2,) + given[3].shape, jnp.bfloat16)],
    )(given[0], *in_vmem(*given[1:]))


def correction(*given):
    return pl.pallas_call(
        last_kernel,
        out_shape=jax.ShapeDtypeStruct(given[-1].shape, jnp.bfloat16),
        in_specs=[SCALAR] + [WHOLE] * (len(given) - 1),
        out_specs=WHOLE,
        scratch_shapes=[pltpu.VMEM((2,) + given[3].shape, jnp.bfloat16)],
    )(given[0], *in_vmem(*given[1:]))


def local(g_lesser, g_retarded, screened, coupling):
    devices = lax.axis_size(ENERGY)
    slabs = lax.axis_size(SLAB)
    chips = devices // 2
    me = lax.axis_index(ENERGY)
    slab = lax.axis_index(SLAB)
    chip, side, odd = me // 2, me % 2, slab % 2
    place = jnp.stack([chip, side, odd]).astype(jnp.int32)

    lesser = g_lesser[0, 0]
    size, width = lesser.shape
    rows = size // chips
    inter = screened[:, 0]
    inter_other = swap_with(inter, 1)
    first = jnp.where(side == 0, inter, inter_other)
    second = jnp.where(side == 0, inter_other, inter)
    inter_rows = jnp.concatenate([first, second], axis=1)

    mine = [lax.dynamic_slice(lesser, (rows * (chip ^ j), 0), (rows, width)) for j in range(chips)]
    pieces = [mine[0]] + [swap_with(mine[j], 2 * j) for j in range(1, chips)]
    pieces = pieces + [swap_with(x, 1) for x in pieces]
    sigma = convolve(chips, place, inter_rows, pieces)

    link = coupling[0]
    link_before = lax.ppermute(link, SLAB, [(s, s ^ 1) for s in range(slabs)])
    before = [swap_across(sigma[j], 2 * j) for j in range(chips)]
    own = [sigma[0]] + [swap_with(sigma[j], 2 * j) for j in range(1, chips)]
    re, im = first_state(chips, place, link, own, before)

    for s in range(1, slabs - 1, 2):
        early_im = lax.ppermute(im, SLAB, [(s, s + 1)])
        early_re = lax.ppermute(re, SLAB, [(s, s + 2)])
        late = lax.ppermute(jnp.where(odd == 1, re, early_im), SLAB, [(s, s + 1), (s + 1, s + 2)])
        given = (place, link, link_before, re, im, early_im, early_re, late)
        if s + 3 < slabs:
            re, im = next_state(*given)
    return correction(*given, g_retarded[0, 0])[None, None]


def solution(mesh):
    placed = (
        P(ENERGY, SLAB, None, None),
        P(ENERGY, SLAB, None, None),
        P(None, SLAB, ENERGY, None),
        P(SLAB, None, None),
    )
    return jax.shard_map(
        local,
        mesh=mesh,
        in_specs=placed,
        out_specs=P(ENERGY, SLAB, None, None),
        check_vma=False,
    )
```

```python
import functools

import jax
import jax.numpy as jnp
from jax import lax
from jax.experimental import pallas as pl
from jax.experimental.pallas import tpu as pltpu
from jax.sharding import PartitionSpec as P

ENERGY = "energy"
SLAB = "slab"
WHOLE = pl.BlockSpec(memory_space=pltpu.VMEM)


def in_vmem(*arrays):
    return [pltpu.with_memory_space_constraint(x, pltpu.VMEM) for x in arrays]


def swap_with(array, mask):
    devices = lax.axis_size(ENERGY)
    return lax.ppermute(array, ENERGY, [(i, i ^ mask) for i in range(devices)])


def swap_slabs(array, slab_to):
    devices, slabs = lax.axis_size(ENERGY), lax.axis_size(SLAB)
    pairs = []
    for e in range(devices):
        for s in range(slabs):
            to = (e, slab_to[s]) if s in slab_to else (e ^ 1, s)
            pairs.append((e * slabs + s, to[0] * slabs + to[1]))
    return lax.ppermute(array, (ENERGY, SLAB), pairs)


def call(kernel, outs, given, scratch=()):
    outs = [pltpu.VMEM(shape, dtype) for shape, dtype in outs]
    return pl.pallas_call(
        kernel,
        out_shape=outs,
        in_specs=[WHOLE] * len(given),
        out_specs=[WHOLE] * len(outs),
        scratch_shapes=list(scratch),
        compiler_params=pltpu.CompilerParams(vmem_limit_bytes=10 << 20),
    )(*in_vmem(*given))


def conv_kernel(chips, inter_ref, *refs):
    pieces = refs[: 2 * chips]
    out_ref, a_ref, b_ref, w_ref, v_ref, sum_ref = refs[2 * chips :]
    me = lax.axis_index(ENERGY)
    chip, side = me // 2, me % 2
    rows, width = inter_ref.shape[1:]
    half = width // 2
    left = lax.broadcasted_iota(jnp.int32, (rows, width), 1) < half

    def swapped(x):
        return jnp.concatenate([x[:, half:], x[:, :half]], axis=1)

    @pl.when(side == 0)
    def _():
        a_ref[0] = jnp.zeros((rows, width), jnp.float32)
        b_ref[0] = jnp.zeros((rows, width), jnp.float32)

    for other in range(2):
        for j in range(chips):
            x = pieces[other * chips + j][...].astype(jnp.float32)
            y = swapped(x)
            slot = 2 * (chip ^ j) + (side ^ other) + 1 - side
            a_ref[slot] = jnp.where(left, x, y)
            b_ref[slot] = jnp.where(left, y, x)
    for m in range(2 * chips):
        x = inter_ref[m].astype(jnp.float32)
        y = swapped(x)
        w_ref[m] = x
        v_ref[m] = jnp.where(left, -y, y)

    step = 8 if rows % 8 == 0 else rows
    lanes = 128 if width % 128 == 0 else width

    def tile(t, carry):
        here = pl.ds(pl.multiple_of(t * step, step), step)
        for c in range(0, width, lanes):
            at = pl.ds(c, lanes)
            for j in range(chips):
                total = None
                for m in range(2 * j + 2):
                    s = 2 * j + 1 - m
                    term = a_ref[s, here, at] * v_ref[m, here, at] - b_ref[s, here, at] * w_ref[m, here, at]
                    total = term if total is None else total + term
                sum_ref[chip ^ j, here, at] = total
        return carry

    lax.fori_loop(0, rows // step, tile, 0)
    out_ref[...] = sum_ref[...].astype(jnp.bfloat16)


def convolve(chips, inter, pieces):
    count, rows, width = inter.shape
    block = lambda n: pltpu.VMEM((n, rows, width), jnp.float32)
    return pl.pallas_call(
        functools.partial(conv_kernel, chips),
        out_shape=pltpu.VMEM((chips, rows, width), jnp.bfloat16),
        in_specs=[WHOLE] * (1 + 2 * chips),
        out_specs=WHOLE,
        scratch_shapes=[block(count + 1), block(count + 1), block(count), block(count), block(chips)],
        compiler_params=pltpu.CompilerParams(vmem_limit_bytes=16 << 20),
        cost_estimate=pl.CostEstimate(flops=count * count * rows * width * 4, bytes_accessed=0, transcendentals=0),
    )(*in_vmem(inter, *pieces))


def dot(a, b):
    return jnp.dot(a, b, preferred_element_type=jnp.float32)


def packed(x):
    half = x.shape[0] // 2
    return jnp.concatenate([x[:half], x[half:]], axis=1)


def unpacked(x):
    size = x.shape[1] // 2
    return jnp.concatenate([x[:, :size], x[:, size:]], axis=0)


def moved(link_ref, turned_ref, x):
    return dot(dot(link_ref[...], x).astype(jnp.bfloat16), turned_ref[...])


def gather_kernel(*refs):
    chip = lax.axis_index(ENERGY) // 2
    first_ref, *others, re_ref, im_ref, all_ref = refs
    chips, rows, width = all_ref.shape
    half = width // 2
    for j, piece in enumerate([first_ref[0], *(ref[...] for ref in others)]):
        all_ref[chip ^ j] = piece
    whole = all_ref[...].reshape(chips * rows, width)
    re_ref[...] = packed(whole[:, :half])
    im_ref[...] = packed(whole[:, half:])


def gathered(own, pieces):
    chips, rows, width = own.shape
    part = ((chips * rows // 2, width), jnp.bfloat16)
    return call(gather_kernel, [part, part], [own, *pieces], [pltpu.VMEM(own.shape, own.dtype)])


def prepare_kernel(link_ref, before_ref, green_ref, turned_ref, step_ref, turned_step_ref, stack_ref, first_ref, second_ref):
    odd = lax.axis_index(SLAB) % 2
    turned_ref[...] = link_ref[...].T

    @pl.when(odd == 0)
    def _():
        step_ref[...] = link_ref[...]

    @pl.when(odd == 1)
    def _():
        step_ref[...] = dot(link_ref[...], before_ref[...]).astype(jnp.bfloat16)

    turned_step_ref[...] = step_ref[...].T
    size = green_ref.shape[0]
    re, im = green_ref[:, :size], green_ref[:, size:]
    stack_ref[:size] = re
    stack_ref[size:] = im
    first_ref[...] = jnp.concatenate([re, -im], axis=0).T
    second_ref[...] = jnp.concatenate([im, re], axis=0).T


def carry_in(turn, link_ref, turned_ref, state_ref, came, out_ref):
    @pl.when(turn)
    def _():
        state = unpacked(state_ref[...]).astype(jnp.float32)
        out_ref[...] = packed((state + moved(link_ref, turned_ref, unpacked(came))).astype(jnp.bfloat16))

    @pl.when(jnp.logical_not(turn))
    def _():
        out_ref[...] = state_ref[...]


def first_kernel(link_ref, turned_ref, own_ref, came_ref, out_ref):
    carry_in(lax.axis_index(SLAB) % 2 == 1, link_ref, turned_ref, own_ref, came_ref[...], out_ref)


def advance_kernel(pair, step_ref, turned_ref, state_ref, near_ref, far_ref, out_ref):
    slab = lax.axis_index(SLAB)
    came = jnp.where(slab % 2 == 0, near_ref[...], far_ref[...])
    carry_in(slab // 2 == pair, step_ref, turned_ref, state_ref, came, out_ref)


def early_kernel(pair, step_ref, turned_ref, stack_ref, re_ref, near_ref, far_ref, out_ref, x_ref):
    advance_kernel(pair, step_ref, turned_ref, re_ref, near_ref, far_ref, x_ref)
    out_ref[...] = dot(stack_ref[...], unpacked(x_ref[...]))


def late_kernel(pair, step_ref, turned_ref, stack_ref, first_ref, second_ref, im_ref, near_ref, far_ref, early_ref, out_ref, x_ref):
    advance_kernel(pair, step_ref, turned_ref, im_ref, near_ref, far_ref, x_ref)
    late = dot(stack_ref[...], unpacked(x_ref[...]))
    size = x_ref.shape[1] // 2
    left_re = (early_ref[:size] - late[size:]).astype(jnp.bfloat16)
    left_im = (late[:size] + early_ref[size:]).astype(jnp.bfloat16)
    out_ref[...] = (dot(left_re, first_ref[...]) + dot(left_im, second_ref[...])).astype(jnp.bfloat16)


def local(g_lesser, g_retarded, screened, coupling):
    devices = lax.axis_size(ENERGY)
    slabs = lax.axis_size(SLAB)
    chips = devices // 2
    me = lax.axis_index(ENERGY)
    chip, side = me // 2, me % 2

    lesser = g_lesser[0, 0]
    size, width = lesser.shape
    rows = size // chips
    inter = screened[:, 0]
    inter_other = swap_with(inter, 1)
    first = jnp.where(side == 0, inter, inter_other)
    second = jnp.where(side == 0, inter_other, inter)
    inter_rows = jnp.concatenate([first, second], axis=1)

    link = coupling[0]
    other_in_pair = {s: s ^ 1 for s in range(slabs)}
    link_before = swap_slabs(link, other_in_pair)
    square = (link.shape, jnp.bfloat16)
    tall, wide = ((2 * size, size), jnp.bfloat16), ((size, 2 * size), jnp.bfloat16)
    prepared = call(prepare_kernel, [square, square, square, tall, wide, wide], [link, link_before, g_retarded[0, 0]])

    mine = [lax.dynamic_slice(lesser, (rows * (chip ^ j), 0), (rows, width)) for j in range(chips)]
    pieces = [mine[0]] + [swap_with(mine[j], 2 * j) for j in range(1, chips)]
    pieces = pieces + [swap_with(x, 1) for x in pieces]
    inter_rows, prepared = lax.optimization_barrier((inter_rows, prepared))
    turned, step, turned_step, stack, adjoint_first, adjoint_second = prepared
    sigma = convolve(chips, inter_rows, pieces)

    own_re, own_im = gathered(sigma, [swap_with(sigma[j], 2 * j) for j in range(1, chips)])
    part = (own_re.shape, own_re.dtype)
    came_re = swap_slabs(own_re, other_in_pair)
    own_im, came_re = lax.optimization_barrier((own_im, came_re))
    came_im = swap_slabs(own_im, other_in_pair)
    (re,) = call(first_kernel, [part], [link, turned, own_re, came_re])
    (im,) = call(first_kernel, [part], [link, turned, own_im, came_im])

    for s in range(1, slabs - 1, 2):
        pair = (s + 1) // 2
        near_re = swap_slabs(re, {s: s + 1, s + 1: s})
        near_im = swap_slabs(im, {s: s + 1, s + 1: s})
        far_re = swap_slabs(near_re, {s + 1: s + 2, s + 2: s + 1})
        far_im = swap_slabs(near_im, {s + 1: s + 2, s + 2: s + 1})
        if s + 3 < slabs:
            advance = functools.partial(advance_kernel, pair)
            (re,) = call(advance, [part], [step, turned_step, re, near_re, far_re])
            (im,) = call(advance, [part], [step, turned_step, im, near_im, far_im])
    scratch = pltpu.VMEM(re.shape, jnp.bfloat16)
    (early,) = call(
        functools.partial(early_kernel, pair),
        [((2 * size, size), jnp.float32)],
        [step, turned_step, stack, re, near_re, far_re],
        [scratch],
    )
    given = [step, turned_step, stack, adjoint_first, adjoint_second, im, near_im, far_im, early]
    out = pl.pallas_call(
        functools.partial(late_kernel, pair),
        out_shape=jax.ShapeDtypeStruct((size, width), jnp.bfloat16),
        in_specs=[WHOLE] * len(given),
        out_specs=WHOLE,
        scratch_shapes=[scratch],
        compiler_params=pltpu.CompilerParams(vmem_limit_bytes=10 << 20),
    )(*in_vmem(*given))
    return out[None, None]


def solution(mesh):
    placed = (
        P(ENERGY, SLAB, None, None),
        P(ENERGY, SLAB, None, None),
        P(None, SLAB, ENERGY, None),
        P(SLAB, None, None),
    )
    return jax.shard_map(
        local,
        mesh=mesh,
        in_specs=placed,
        out_specs=P(ENERGY, SLAB, None, None),
        check_vma=False,
    )
```

```python
import functools

import jax
import jax.numpy as jnp
from jax import lax
from jax.experimental import pallas as pl
from jax.experimental.pallas import tpu as pltpu
from jax.sharding import PartitionSpec as P

ENERGY = "energy"
SLAB = "slab"
WHOLE = pl.BlockSpec(memory_space=pltpu.VMEM)


def in_vmem(*arrays):
    return [pltpu.with_memory_space_constraint(x, pltpu.VMEM) for x in arrays]


def swap_with(array, mask):
    devices = lax.axis_size(ENERGY)
    return lax.ppermute(array, ENERGY, [(i, i ^ mask) for i in range(devices)])


def swap_slabs(array, slab_to):
    devices, slabs = lax.axis_size(ENERGY), lax.axis_size(SLAB)
    pairs = []
    for e in range(devices):
        for s in range(slabs):
            to = (e, slab_to[s]) if s in slab_to else (e ^ 1, s)
            pairs.append((e * slabs + s, to[0] * slabs + to[1]))
    return lax.ppermute(array, (ENERGY, SLAB), pairs)


def call(kernel, outs, given, scratch=()):
    outs = [pltpu.VMEM(shape, dtype) for shape, dtype in outs]
    return pl.pallas_call(
        kernel,
        out_shape=outs,
        in_specs=[WHOLE] * len(given),
        out_specs=[WHOLE] * len(outs),
        scratch_shapes=list(scratch),
        compiler_params=pltpu.CompilerParams(vmem_limit_bytes=10 << 20),
    )(*in_vmem(*given))


def conv_kernel(chips, inter_ref, *refs):
    pieces = refs[: 2 * chips]
    out_ref, a_ref, b_ref, w_ref, v_ref, sum_ref = refs[2 * chips :]
    me = lax.axis_index(ENERGY)
    chip, side = me // 2, me % 2
    rows, width = inter_ref.shape[1:]
    half = width // 2
    left = lax.broadcasted_iota(jnp.int32, (rows, width), 1) < half

    def swapped(x):
        return jnp.concatenate([x[:, half:], x[:, :half]], axis=1)

    @pl.when(side == 0)
    def _():
        a_ref[0] = jnp.zeros((rows, width), jnp.float32)
        b_ref[0] = jnp.zeros((rows, width), jnp.float32)

    for other in range(2):
        for j in range(chips):
            x = pieces[other * chips + j][...].astype(jnp.float32)
            y = swapped(x)
            slot = 2 * (chip ^ j) + (side ^ other) + 1 - side
            a_ref[slot] = jnp.where(left, x, y)
            b_ref[slot] = jnp.where(left, y, x)
    for m in range(2 * chips):
        x = inter_ref[m].astype(jnp.float32)
        y = swapped(x)
        w_ref[m] = x
        v_ref[m] = jnp.where(left, -y, y)

    step = 8 if rows % 8 == 0 else rows
    lanes = 128 if width % 128 == 0 else width

    def tile(t, carry):
        here = pl.ds(pl.multiple_of(t * step, step), step)
        for c in range(0, width, lanes):
            at = pl.ds(c, lanes)
            for j in range(chips):
                total = None
                for m in range(2 * j + 2):
                    s = 2 * j + 1 - m
                    term = a_ref[s, here, at] * v_ref[m, here, at] - b_ref[s, here, at] * w_ref[m, here, at]
                    total = term if total is None else total + term
                sum_ref[chip ^ j, here, at] = total
        return carry

    lax.fori_loop(0, rows // step, tile, 0)
    out_ref[...] = sum_ref[...].astype(jnp.bfloat16)


def convolve(chips, inter, pieces):
    count, rows, width = inter.shape
    block = lambda n: pltpu.VMEM((n, rows, width), jnp.float32)
    return pl.pallas_call(
        functools.partial(conv_kernel, chips),
        out_shape=pltpu.VMEM((chips, rows, width), jnp.bfloat16),
        in_specs=[WHOLE] * (1 + 2 * chips),
        out_specs=WHOLE,
        scratch_shapes=[block(count + 1), block(count + 1), block(count), block(count), block(chips)],
        compiler_params=pltpu.CompilerParams(vmem_limit_bytes=16 << 20),
        cost_estimate=pl.CostEstimate(flops=count * count * rows * width * 4, bytes_accessed=0, transcendentals=0),
    )(*in_vmem(inter, *pieces))


def dot(a, b):
    return jnp.dot(a, b, preferred_element_type=jnp.float32)


def packed(x):
    half = x.shape[0] // 2
    return jnp.concatenate([x[:half], x[half:]], axis=1)


def unpacked(x):
    size = x.shape[1] // 2
    return jnp.concatenate([x[:, :size], x[:, size:]], axis=0)


def moved(link_ref, turned_ref, x):
    return dot(dot(link_ref[...], x).astype(jnp.bfloat16), turned_ref[...])


def gather_kernel(*refs):
    chip = lax.axis_index(ENERGY) // 2
    first_ref, *others, re_ref, im_ref, all_ref = refs
    all_ref[chip] = first_ref[0]
    for j, ref in enumerate(others):
        all_ref[chip ^ (j + 1)] = ref[...]
    chips, rows, width = all_ref.shape
    whole = all_ref[...].reshape(chips * rows, width)
    re_ref[...] = packed(whole[:, : width // 2])
    im_ref[...] = packed(whole[:, width // 2 :])


def gathered(own, pieces):
    chips, rows, width = own.shape
    part = ((chips * rows // 2, width), jnp.bfloat16)
    return call(gather_kernel, [part, part], [own, *pieces], [pltpu.VMEM(own.shape, own.dtype)])


def adjoint(stack, sign):
    size = stack.shape[1]
    re, im = stack[:size], stack[size:]
    return jnp.concatenate([re, -im] if sign > 0 else [im, re], axis=0).T


def prepare_kernel(pair, link_ref, before_ref, green_ref, turned_ref, step_ref, turned_step_ref, *refs):
    stack_ref, first_ref, second_ref, far_stack_ref, far_first_ref, far_second_ref, half_a_ref, half_b_ref = refs
    slab = lax.axis_index(SLAB)
    turned_ref[...] = link_ref[...].T

    @pl.when(slab % 2 == 0)
    def _():
        step_ref[...] = link_ref[...]

    @pl.when(slab % 2 == 1)
    def _():
        step_ref[...] = dot(link_ref[...], before_ref[...]).astype(jnp.bfloat16)

    turned_step_ref[...] = step_ref[...].T
    size = green_ref.shape[0]
    stack_ref[:size] = green_ref[:, :size]
    stack_ref[size:] = green_ref[:, size:]
    first_ref[...] = adjoint(stack_ref[...], 1)
    second_ref[...] = adjoint(stack_ref[...], -1)

    @pl.when(slab // 2 == pair)
    def _():
        far_stack_ref[...] = dot(stack_ref[...], step_ref[...]).astype(jnp.bfloat16)
        far_first_ref[...] = adjoint(far_stack_ref[...], 1)
        far_second_ref[...] = adjoint(far_stack_ref[...], -1)
        quarter = size // 4
        columns = [far_stack_ref[:, i * quarter : (i + 1) * quarter] for i in range(4)]
        half_a_ref[...] = jnp.concatenate([columns[0], columns[2]], axis=1)
        half_b_ref[...] = jnp.concatenate([columns[1], columns[3]], axis=1)


def joined(refs):
    return jnp.concatenate([ref[...] for ref in refs], axis=0)


def carry_in(turn, link_ref, turned_ref, state, came, out_refs):
    rows = out_refs[0].shape[0]

    @pl.when(turn)
    def _():
        out = (unpacked(state).astype(jnp.float32) + moved(link_ref, turned_ref, unpacked(came))).astype(jnp.bfloat16)
        out = packed(out)
        for i, ref in enumerate(out_refs):
            ref[...] = out[i * rows : (i + 1) * rows]

    @pl.when(jnp.logical_not(turn))
    def _():
        for i, ref in enumerate(out_refs):
            ref[...] = state[i * rows : (i + 1) * rows]


def first_kernel(link_ref, turned_ref, own_ref, came_ref, *out_refs):
    carry_in(lax.axis_index(SLAB) % 2 == 1, link_ref, turned_ref, own_ref[...], came_ref[...], out_refs)


def arrived(refs):
    near, far = refs[: len(refs) // 2], refs[len(refs) // 2 :]
    return jnp.where(lax.axis_index(SLAB) % 2 == 0, joined(near), joined(far))


def advance_kernel(pair, link_ref, turned_ref, *refs):
    parts = len(refs) // 4
    state, came, outs = refs[:parts], refs[parts : 3 * parts], refs[3 * parts :]
    carry_in(lax.axis_index(SLAB) // 2 == pair, link_ref, turned_ref, joined(state), arrived(came), outs)


def base_kernel(stack_ref, first_ref, second_ref, re_ref, *refs):
    *im_refs, out_ref = refs
    re = dot(stack_ref[...], unpacked(re_ref[...]))
    im = dot(stack_ref[...], unpacked(joined(im_refs)))
    size = re.shape[1]
    left_re = (re[:size] - im[size:]).astype(jnp.bfloat16)
    left_im = (im[:size] + re[size:]).astype(jnp.bfloat16)
    out_ref[...] = dot(left_re, first_ref[...]) + dot(left_im, second_ref[...])


def early_kernel(pair, far_stack_ref, far_first_ref, far_second_ref, half_ref, base_ref, *refs):
    *came, out_ref, left_ref = refs
    turn = lax.axis_index(SLAB) // 2 == pair

    @pl.when(turn)
    def _():
        left = dot(far_stack_ref[...], unpacked(arrived(came[::2]))).astype(jnp.bfloat16)
        size = left.shape[1]
        out_ref[...] = base_ref[...] + dot(left[:size], far_first_ref[...]) + dot(left[size:], far_second_ref[...])
        left_ref[...] = dot(half_ref[...], unpacked(arrived(came[1::2])))

    @pl.when(jnp.logical_not(turn))
    def _():
        out_ref[...] = base_ref[...]


def late_kernel(pair, far_first_ref, far_second_ref, half_ref, early_ref, early_left_ref, *refs):
    *came, out_ref, left_ref, result_ref, sems = refs
    size, width = result_ref.shape
    turn = lax.axis_index(SLAB) // 2 == pair
    cut = width // 256 * 128 if width % 128 == 0 else width // 2

    @pl.when(turn)
    def _():
        left_ref[...] = (early_left_ref[...] + dot(half_ref[...], unpacked(arrived(came)))).astype(jnp.bfloat16)

    copies = []
    for n, block in enumerate((slice(0, cut), slice(cut, width))):

        @pl.when(turn)
        def _():
            late = dot(left_ref[:size], far_second_ref[:, block]) - dot(left_ref[size:], far_first_ref[:, block])
            result_ref[:, block] = (early_ref[:, block] + late).astype(jnp.bfloat16)

        @pl.when(jnp.logical_not(turn))
        def _():
            result_ref[:, block] = early_ref[:, block].astype(jnp.bfloat16)

        copy = pltpu.make_async_copy(result_ref.at[:, block], out_ref.at[:, block], sems.at[n])
        copy.start()
        copies.append(copy)
    for copy in copies:
        copy.wait()


def local(g_lesser, g_retarded, screened, coupling):
    devices = lax.axis_size(ENERGY)
    slabs = lax.axis_size(SLAB)
    chips = devices // 2
    me = lax.axis_index(ENERGY)
    chip, side = me // 2, me % 2

    lesser = g_lesser[0, 0]
    size, width = lesser.shape
    rows = size // chips
    inter = screened[:, 0]
    inter_other = swap_with(inter, 1)
    first = jnp.where(side == 0, inter, inter_other)
    second = jnp.where(side == 0, inter_other, inter)
    inter_rows = jnp.concatenate([first, second], axis=1)

    mine = [lax.dynamic_slice(lesser, (rows * (chip ^ j), 0), (rows, width)) for j in range(chips)]
    pieces = [mine[0]] + [swap_with(mine[j], 2 * j) for j in range(1, chips)]

    link = coupling[0]
    other_in_pair = {s: s ^ 1 for s in range(slabs)}
    link_before = swap_slabs(link, other_in_pair)

    pieces = pieces + [swap_with(x, 1) for x in pieces]
    sigma = convolve(chips, inter_rows, pieces)
    sigma, link_before = lax.optimization_barrier((sigma, link_before))
    own_re, own_im = gathered(sigma, [swap_with(sigma[j], 2 * j) for j in range(1, chips)])

    own_re, own_im, link_before = lax.optimization_barrier((own_re, own_im, link_before))
    square = (link.shape, jnp.bfloat16)
    tall, wide = ((2 * size, size), jnp.bfloat16), ((size, 2 * size), jnp.bfloat16)
    thin = ((2 * size, size // 2), jnp.bfloat16)
    last_pair = slabs // 2 - 1
    prepared = call(
        functools.partial(prepare_kernel, last_pair),
        [square, square, square, tall, wide, wide, tall, wide, wide, thin, thin],
        [link, link_before, g_retarded[0, 0]],
    )
    turned, step, turned_step, *base, far_stack, far_first, far_second, half_a, half_b = prepared
    came_re = swap_slabs(own_re, other_in_pair)
    came_im = swap_slabs(own_im, other_in_pair)
    part = (own_re.shape, own_re.dtype)
    halves = [((size // 4, width), own_im.dtype)] * 2
    total = [((size, width), jnp.float32)]
    re = call(first_kernel, [part], [link, turned, own_re, came_re])
    im = call(first_kernel, halves, [link, turned, own_im, came_im])

    for s in range(1, slabs - 1, 2):
        pair = (s + 1) // 2
        near, far = {s: s + 1, s + 1: s}, {s + 1: s + 2, s + 2: s + 1}
        near_re = [swap_slabs(x, near) for x in re]
        near_im = [swap_slabs(x, near) for x in im]
        far_re = [swap_slabs(x, far) for x in near_re]
        far_im = [swap_slabs(x, far) for x in near_im]
        if pair < last_pair:
            advance = functools.partial(advance_kernel, pair)
            re = call(advance, [part], [step, turned_step, *re, *near_re, *far_re])
            im = call(advance, halves, [step, turned_step, *im, *near_im, *far_im])
    (out,) = call(base_kernel, total, [*base, *re, *im])
    early = [far_stack, far_first, far_second, half_a, out, near_re[0], near_im[0], far_re[0], far_im[0]]
    left = ((2 * size, size), jnp.float32)
    out, left = call(functools.partial(early_kernel, last_pair), [*total, left], early)
    given = [far_first, far_second, half_b, out, left, near_im[1], far_im[1]]
    out = pl.pallas_call(
        functools.partial(late_kernel, last_pair),
        out_shape=jax.ShapeDtypeStruct((size, width), jnp.bfloat16),
        in_specs=[WHOLE] * len(given),
        out_specs=pl.BlockSpec(memory_space=pl.ANY),
        scratch_shapes=[
            pltpu.VMEM((2 * size, size), jnp.bfloat16),
            pltpu.VMEM((size, width), jnp.bfloat16),
            pltpu.SemaphoreType.DMA((2,)),
        ],
        compiler_params=pltpu.CompilerParams(vmem_limit_bytes=10 << 20),
    )(*in_vmem(*given))
    return out[None, None]


def solution(mesh):
    placed = (
        P(ENERGY, SLAB, None, None),
        P(ENERGY, SLAB, None, None),
        P(None, SLAB, ENERGY, None),
        P(SLAB, None, None),
    )
    return jax.shard_map(
        local,
        mesh=mesh,
        in_specs=placed,
        out_specs=P(ENERGY, SLAB, None, None),
        check_vma=False,
    )
```

```python
import functools

import jax
import jax.numpy as jnp
from jax import lax
from jax.experimental import pallas as pl
from jax.experimental.pallas import tpu as pltpu
from jax.sharding import PartitionSpec as P

ENERGY = "energy"
SLAB = "slab"
WHOLE = pl.BlockSpec(memory_space=pltpu.VMEM)


def in_vmem(*arrays):
    return [pltpu.with_memory_space_constraint(x, pltpu.VMEM) for x in arrays]


def swap_with(array, mask):
    devices = lax.axis_size(ENERGY)
    return lax.ppermute(array, ENERGY, [(i, i ^ mask) for i in range(devices)])


def swap_slabs(array, slab_to):
    devices, slabs = lax.axis_size(ENERGY), lax.axis_size(SLAB)
    pairs = []
    for e in range(devices):
        for s in range(slabs):
            to = (e, slab_to[s]) if s in slab_to else (e ^ (2 if s % 2 else 4), s)
            pairs.append((e * slabs + s, to[0] * slabs + to[1]))
    return lax.ppermute(array, (ENERGY, SLAB), pairs)


def call(kernel, outs, given, scratch=()):
    outs = [pltpu.VMEM(shape, dtype) for shape, dtype in outs]
    return pl.pallas_call(
        kernel,
        out_shape=outs,
        in_specs=[WHOLE] * len(given),
        out_specs=[WHOLE] * len(outs),
        scratch_shapes=list(scratch),
        compiler_params=pltpu.CompilerParams(vmem_limit_bytes=10 << 20),
    )(*in_vmem(*given))


def conv_kernel(chips, inter_ref, *refs):
    pieces = refs[: 2 * chips]
    out_ref, a_ref, b_ref, w_ref, v_ref, sum_ref = refs[2 * chips :]
    me = lax.axis_index(ENERGY)
    chip, side = me // 2, me % 2
    rows, width = inter_ref.shape[1:]
    half = width // 2
    left = lax.broadcasted_iota(jnp.int32, (rows, width), 1) < half

    def swapped(x):
        return jnp.concatenate([x[:, half:], x[:, :half]], axis=1)

    @pl.when(side == 0)
    def _():
        a_ref[0] = jnp.zeros((rows, width), jnp.float32)
        b_ref[0] = jnp.zeros((rows, width), jnp.float32)

    for other in range(2):
        for j in range(chips):
            x = pieces[other * chips + j][...].astype(jnp.float32)
            y = swapped(x)
            slot = 2 * (chip ^ j) + (side ^ other) + 1 - side
            a_ref[slot] = jnp.where(left, x, y)
            b_ref[slot] = jnp.where(left, y, x)
    for m in range(2 * chips):
        x = inter_ref[m].astype(jnp.float32)
        y = swapped(x)
        w_ref[m] = x
        v_ref[m] = jnp.where(left, -y, y)

    step = 8 if rows % 8 == 0 else rows
    lanes = 128 if width % 128 == 0 else width

    def tile(t, carry):
        here = pl.ds(pl.multiple_of(t * step, step), step)
        for c in range(0, width, lanes):
            at = pl.ds(c, lanes)
            for j in range(chips):
                total = None
                for m in range(2 * j + 2):
                    s = 2 * j + 1 - m
                    term = a_ref[s, here, at] * v_ref[m, here, at] - b_ref[s, here, at] * w_ref[m, here, at]
                    total = term if total is None else total + term
                sum_ref[chip ^ j, here, at] = total
        return carry

    lax.fori_loop(0, rows // step, tile, 0)
    out_ref[...] = sum_ref[...].astype(jnp.bfloat16)


def convolve(chips, inter, pieces):
    count, rows, width = inter.shape
    block = lambda n: pltpu.VMEM((n, rows, width), jnp.float32)
    return pl.pallas_call(
        functools.partial(conv_kernel, chips),
        out_shape=pltpu.VMEM((chips, rows, width), jnp.bfloat16),
        in_specs=[WHOLE] * (1 + 2 * chips),
        out_specs=WHOLE,
        scratch_shapes=[block(count + 1), block(count + 1), block(count), block(count), block(chips)],
        compiler_params=pltpu.CompilerParams(vmem_limit_bytes=16 << 20),
        cost_estimate=pl.CostEstimate(flops=count * count * rows * width * 4, bytes_accessed=0, transcendentals=0),
    )(*in_vmem(inter, *pieces))


def dot(a, b):
    return jnp.dot(a, b, preferred_element_type=jnp.float32)


def packed(x):
    half = x.shape[0] // 2
    return jnp.concatenate([x[:half], x[half:]], axis=1)


def unpacked(x):
    size = x.shape[1] // 2
    return jnp.concatenate([x[:, :size], x[:, size:]], axis=0)


def moved(link_ref, turned_ref, x):
    return dot(dot(link_ref[...], x).astype(jnp.bfloat16), turned_ref[...])


def gather_kernel(*refs):
    chip = lax.axis_index(ENERGY) // 2
    first_ref, *others, re_ref, im_ref, all_ref = refs
    all_ref[chip] = first_ref[0]
    for j, ref in enumerate(others):
        all_ref[chip ^ (j + 1)] = ref[...]
    chips, rows, width = all_ref.shape
    whole = all_ref[...].reshape(chips * rows, width)
    re_ref[...] = packed(whole[:, : width // 2])
    im_ref[...] = packed(whole[:, width // 2 :])


def gathered(own, pieces):
    chips, rows, width = own.shape
    part = ((chips * rows // 2, width), jnp.bfloat16)
    return call(gather_kernel, [part, part], [own, *pieces], [pltpu.VMEM(own.shape, own.dtype)])


def adjoint(stack, sign):
    size = stack.shape[1]
    re, im = stack[:size], stack[size:]
    return jnp.concatenate([re, -im] if sign > 0 else [im, re], axis=0).T


def prepare_kernel(pair, link_ref, before_ref, green_ref, turned_ref, step_ref, turned_step_ref, *refs):
    stack_ref, first_ref, second_ref, far_stack_ref, far_first_ref, far_second_ref, half_a_ref, half_b_ref = refs
    slab = lax.axis_index(SLAB)
    turned_ref[...] = link_ref[...].T

    @pl.when(slab % 2 == 0)
    def _():
        step_ref[...] = link_ref[...]

    @pl.when(slab % 2 == 1)
    def _():
        step_ref[...] = dot(link_ref[...], before_ref[...]).astype(jnp.bfloat16)

    turned_step_ref[...] = step_ref[...].T
    size = green_ref.shape[0]
    stack_ref[:size] = green_ref[:, :size]
    stack_ref[size:] = green_ref[:, size:]
    first_ref[...] = adjoint(stack_ref[...], 1)
    second_ref[...] = adjoint(stack_ref[...], -1)

    @pl.when(slab // 2 == pair)
    def _():
        far_stack_ref[...] = dot(stack_ref[...], step_ref[...]).astype(jnp.bfloat16)
        far_first_ref[...] = adjoint(far_stack_ref[...], 1)
        far_second_ref[...] = adjoint(far_stack_ref[...], -1)
        quarter = size // 4
        columns = [far_stack_ref[:, i * quarter : (i + 1) * quarter] for i in range(4)]
        half_a_ref[...] = jnp.concatenate([columns[0], columns[2]], axis=1)
        half_b_ref[...] = jnp.concatenate([columns[1], columns[3]], axis=1)


def joined(refs):
    return jnp.concatenate([ref[...] for ref in refs], axis=0)


def carry_in(turn, link_ref, turned_ref, state, came, out_refs):
    rows = out_refs[0].shape[0]

    @pl.when(turn)
    def _():
        out = (unpacked(state).astype(jnp.float32) + moved(link_ref, turned_ref, unpacked(came))).astype(jnp.bfloat16)
        out = packed(out)
        for i, ref in enumerate(out_refs):
            ref[...] = out[i * rows : (i + 1) * rows]

    @pl.when(jnp.logical_not(turn))
    def _():
        for i, ref in enumerate(out_refs):
            ref[...] = state[i * rows : (i + 1) * rows]


def first_kernel(link_ref, turned_ref, own_ref, came_ref, *out_refs):
    carry_in(lax.axis_index(SLAB) % 2 == 1, link_ref, turned_ref, own_ref[...], came_ref[...], out_refs)


def arrived(refs):
    near, far = refs[: len(refs) // 2], refs[len(refs) // 2 :]
    return jnp.where(lax.axis_index(SLAB) % 2 == 0, joined(near), joined(far))


def advance_kernel(pair, link_ref, turned_ref, *refs):
    parts = len(refs) // 4
    state, came, outs = refs[:parts], refs[parts : 3 * parts], refs[3 * parts :]
    carry_in(lax.axis_index(SLAB) // 2 == pair, link_ref, turned_ref, joined(state), arrived(came), outs)


def base_kernel(stack_ref, first_ref, second_ref, *refs):
    *state, out_ref = refs
    re = dot(stack_ref[...], unpacked(joined(state[:2])))
    im = dot(stack_ref[...], unpacked(joined(state[2:])))
    size = re.shape[1]
    left_re = (re[:size] - im[size:]).astype(jnp.bfloat16)
    left_im = (im[:size] + re[size:]).astype(jnp.bfloat16)
    out_ref[...] = dot(left_re, first_ref[...]) + dot(left_im, second_ref[...])


def early_kernel(pair, far_stack_ref, far_first_ref, far_second_ref, base_ref, *refs):
    *came, out_ref = refs
    turn = lax.axis_index(SLAB) // 2 == pair

    @pl.when(turn)
    def _():
        left = dot(far_stack_ref[...], unpacked(arrived(came))).astype(jnp.bfloat16)
        size = left.shape[1]
        out_ref[...] = base_ref[...] + dot(left[:size], far_first_ref[...]) + dot(left[size:], far_second_ref[...])

    @pl.when(jnp.logical_not(turn))
    def _():
        out_ref[...] = base_ref[...]


def half_kernel(pair, half_ref, *refs):
    *came, left_ref = refs

    @pl.when(lax.axis_index(SLAB) // 2 == pair)
    def _():
        left_ref[...] = dot(half_ref[...], unpacked(arrived(came)))


def late_kernel(pair, far_first_ref, far_second_ref, half_ref, early_ref, early_left_ref, *refs):
    *came, out_ref, left_ref, result_ref, sems = refs
    size, width = result_ref.shape
    turn = lax.axis_index(SLAB) // 2 == pair
    cut = width // 256 * 128 if width % 128 == 0 else width // 2

    @pl.when(turn)
    def _():
        left_ref[...] = (early_left_ref[...] + dot(half_ref[...], unpacked(arrived(came)))).astype(jnp.bfloat16)

    copies = []
    for n, block in enumerate((slice(0, cut), slice(cut, width))):

        @pl.when(turn)
        def _():
            late = dot(left_ref[:size], far_second_ref[:, block]) - dot(left_ref[size:], far_first_ref[:, block])
            result_ref[:, block] = (early_ref[:, block] + late).astype(jnp.bfloat16)

        @pl.when(jnp.logical_not(turn))
        def _():
            result_ref[:, block] = early_ref[:, block].astype(jnp.bfloat16)

        copy = pltpu.make_async_copy(result_ref.at[:, block], out_ref.at[:, block], sems.at[n])
        copy.start()
        copies.append(copy)
    for copy in copies:
        copy.wait()


def local(g_lesser, g_retarded, screened, coupling):
    devices = lax.axis_size(ENERGY)
    slabs = lax.axis_size(SLAB)
    chips = devices // 2
    me = lax.axis_index(ENERGY)
    chip, side = me // 2, me % 2

    lesser = g_lesser[0, 0]
    size, width = lesser.shape
    rows = size // chips
    inter = screened[:, 0]
    inter_other = swap_with(inter, 1)
    first = jnp.where(side == 0, inter, inter_other)
    second = jnp.where(side == 0, inter_other, inter)
    inter_rows = jnp.concatenate([first, second], axis=1)

    mine = [lax.dynamic_slice(lesser, (rows * (chip ^ j), 0), (rows, width)) for j in range(chips)]
    pieces = [mine[0]] + [swap_with(mine[j], 2 * j) for j in range(1, chips)]

    link = coupling[0]
    other_in_pair = {s: s ^ 1 for s in range(slabs)}
    link_before = swap_slabs(link, other_in_pair)

    pieces = pieces + [swap_with(x, 1) for x in pieces]
    sigma = convolve(chips, inter_rows, pieces)
    sigma, link_before = lax.optimization_barrier((sigma, link_before))
    own_re, own_im = gathered(sigma, [swap_with(sigma[j], 2 * j) for j in range(1, chips)])

    own_re, own_im, link_before = lax.optimization_barrier((own_re, own_im, link_before))
    square = (link.shape, jnp.bfloat16)
    tall, wide = ((2 * size, size), jnp.bfloat16), ((size, 2 * size), jnp.bfloat16)
    thin = ((2 * size, size // 2), jnp.bfloat16)
    last_pair = slabs // 2 - 1
    prepared = call(
        functools.partial(prepare_kernel, last_pair),
        [square, square, square, tall, wide, wide, tall, wide, wide, thin, thin],
        [link, link_before, g_retarded[0, 0]],
    )
    turned, step, turned_step, *base, far_stack, far_first, far_second, half_a, half_b = prepared
    came_re = swap_slabs(own_re, other_in_pair)
    came_im = swap_slabs(own_im, other_in_pair)
    halves = [((size // 4, width), own_im.dtype)] * 2
    total = [((size, width), jnp.float32)]
    re = call(first_kernel, halves, [link, turned, own_re, came_re])
    im = call(first_kernel, halves, [link, turned, own_im, came_im])

    for s in range(1, slabs - 1, 2):
        pair = (s + 1) // 2
        near, far = {s: s + 1, s + 1: s}, other_in_pair
        near_re = [swap_slabs(x, near) for x in re]
        near_im = [swap_slabs(x, near) for x in im]
        far_re = [swap_slabs(x, far) for x in near_re]
        far_im = [swap_slabs(x, far) for x in near_im]
        if pair < last_pair:
            advance = functools.partial(advance_kernel, pair)
            re = call(advance, halves, [step, turned_step, *re, *near_re, *far_re])
            im = call(advance, halves, [step, turned_step, *im, *near_im, *far_im])
    (out,) = call(base_kernel, total, [*base, *re, *im])
    early = [far_stack, far_first, far_second, out, *near_re, *far_re]
    (out,) = call(functools.partial(early_kernel, last_pair), total, early)
    far_im[0], out = lax.optimization_barrier((far_im[0], out))
    left = [((2 * size, size), jnp.float32)]
    (left,) = call(functools.partial(half_kernel, last_pair), left, [half_a, near_im[0], far_im[0]])
    given = [far_first, far_second, half_b, out, left, near_im[1], far_im[1]]
    out = pl.pallas_call(
        functools.partial(late_kernel, last_pair),
        out_shape=jax.ShapeDtypeStruct((size, width), jnp.bfloat16),
        in_specs=[WHOLE] * len(given),
        out_specs=pl.BlockSpec(memory_space=pl.ANY),
        scratch_shapes=[
            pltpu.VMEM((2 * size, size), jnp.bfloat16),
            pltpu.VMEM((size, width), jnp.bfloat16),
            pltpu.SemaphoreType.DMA((2,)),
        ],
        compiler_params=pltpu.CompilerParams(vmem_limit_bytes=10 << 20),
    )(*in_vmem(*given))
    return out[None, None]


def solution(mesh):
    placed = (
        P(ENERGY, SLAB, None, None),
        P(ENERGY, SLAB, None, None),
        P(None, SLAB, ENERGY, None),
        P(SLAB, None, None),
    )
    return jax.shard_map(
        local,
        mesh=mesh,
        in_specs=placed,
        out_specs=P(ENERGY, SLAB, None, None),
        check_vma=False,
    )
```

```python
import functools

import jax
import jax.numpy as jnp
from jax import lax
from jax.experimental import pallas as pl
from jax.experimental.pallas import tpu as pltpu
from jax.sharding import PartitionSpec as P

ENERGY = "energy"
SLAB = "slab"
WHOLE = pl.BlockSpec(memory_space=pltpu.VMEM)


def in_vmem(*arrays):
    return [pltpu.with_memory_space_constraint(x, pltpu.VMEM) for x in arrays]


def swap_with(array, mask):
    devices = lax.axis_size(ENERGY)
    return lax.ppermute(array, ENERGY, [(i, i ^ mask) for i in range(devices)])


def swap_slabs(array, slab_to, idle=1):
    devices, slabs = lax.axis_size(ENERGY), lax.axis_size(SLAB)
    pairs = []
    for e in range(devices):
        for s in range(slabs):
            to = (e, slab_to[s]) if s in slab_to else (e ^ idle, s)
            pairs.append((e * slabs + s, to[0] * slabs + to[1]))
    return lax.ppermute(array, (ENERGY, SLAB), pairs)


def call(kernel, outs, given, scratch=()):
    outs = [pltpu.VMEM(shape, dtype) for shape, dtype in outs]
    return pl.pallas_call(
        kernel,
        out_shape=outs,
        in_specs=[WHOLE] * len(given),
        out_specs=[WHOLE] * len(outs),
        scratch_shapes=list(scratch),
        compiler_params=pltpu.CompilerParams(vmem_limit_bytes=10 << 20),
    )(*in_vmem(*given))


def conv_kernel(chips, inter_ref, *refs):
    pieces = refs[: 2 * chips]
    out_ref, a_ref, b_ref, w_ref, v_ref, sum_ref = refs[2 * chips :]
    me = lax.axis_index(ENERGY)
    chip, side = me // 2, me % 2
    rows, width = inter_ref.shape[1:]
    half = width // 2
    left = lax.broadcasted_iota(jnp.int32, (rows, width), 1) < half

    def swapped(x):
        return jnp.concatenate([x[:, half:], x[:, :half]], axis=1)

    @pl.when(side == 0)
    def _():
        a_ref[0] = jnp.zeros((rows, width), jnp.float32)
        b_ref[0] = jnp.zeros((rows, width), jnp.float32)

    for other in range(2):
        for j in range(chips):
            x = pieces[other * chips + j][...].astype(jnp.float32)
            y = swapped(x)
            slot = 2 * (chip ^ j) + (side ^ other) + 1 - side
            a_ref[slot] = jnp.where(left, x, y)
            b_ref[slot] = jnp.where(left, y, x)
    for m in range(2 * chips):
        x = inter_ref[m].astype(jnp.float32)
        y = swapped(x)
        w_ref[m] = x
        v_ref[m] = jnp.where(left, -y, y)

    step = 8 if rows % 8 == 0 else rows
    lanes = 128 if width % 128 == 0 else width

    def tile(t, carry):
        here = pl.ds(pl.multiple_of(t * step, step), step)
        for c in range(0, width, lanes):
            at = pl.ds(c, lanes)
            for j in range(chips):
                total = None
                for m in range(2 * j + 2):
                    s = 2 * j + 1 - m
                    term = a_ref[s, here, at] * v_ref[m, here, at] - b_ref[s, here, at] * w_ref[m, here, at]
                    total = term if total is None else total + term
                sum_ref[chip ^ j, here, at] = total
        return carry

    lax.fori_loop(0, rows // step, tile, 0)
    out_ref[...] = sum_ref[...].astype(jnp.bfloat16)


def convolve(chips, inter, pieces):
    count, rows, width = inter.shape
    block = lambda n: pltpu.VMEM((n, rows, width), jnp.float32)
    return pl.pallas_call(
        functools.partial(conv_kernel, chips),
        out_shape=pltpu.VMEM((chips, rows, width), jnp.bfloat16),
        in_specs=[WHOLE] * (1 + 2 * chips),
        out_specs=WHOLE,
        scratch_shapes=[block(count + 1), block(count + 1), block(count), block(count), block(chips)],
        compiler_params=pltpu.CompilerParams(vmem_limit_bytes=16 << 20),
        cost_estimate=pl.CostEstimate(flops=count * count * rows * width * 4, bytes_accessed=0, transcendentals=0),
    )(*in_vmem(inter, *pieces))


def dot(a, b):
    return jnp.dot(a, b, preferred_element_type=jnp.float32)


def packed(x):
    half = x.shape[0] // 2
    return jnp.concatenate([x[:half], x[half:]], axis=1)


def unpacked(x):
    size = x.shape[1] // 2
    return jnp.concatenate([x[:, :size], x[:, size:]], axis=0)


def moved(link_ref, turned_ref, x):
    return dot(dot(link_ref[...], x).astype(jnp.bfloat16), turned_ref[...])


def gather_kernel(*refs):
    chip = lax.axis_index(ENERGY) // 2
    first_ref, *others, re_ref, im_ref, all_ref = refs
    all_ref[chip] = first_ref[0]
    for j, ref in enumerate(others):
        all_ref[chip ^ (j + 1)] = ref[...]
    chips, rows, width = all_ref.shape
    whole = all_ref[...].reshape(chips * rows, width)
    re_ref[...] = packed(whole[:, : width // 2])
    im_ref[...] = packed(whole[:, width // 2 :])


def gathered(own, pieces):
    chips, rows, width = own.shape
    part = ((chips * rows // 2, width), jnp.bfloat16)
    return call(gather_kernel, [part, part], [own, *pieces], [pltpu.VMEM(own.shape, own.dtype)])


def adjoint(stack, sign):
    size = stack.shape[1]
    re, im = stack[:size], stack[size:]
    return jnp.concatenate([re, -im] if sign > 0 else [im, re], axis=0).T


def prepare_kernel(pair, link_ref, before_ref, green_ref, turned_ref, step_ref, turned_step_ref, *refs):
    stack_ref, first_ref, second_ref, far_stack_ref, far_first_ref, far_second_ref, half_a_ref, half_b_ref = refs
    slab = lax.axis_index(SLAB)
    turned_ref[...] = link_ref[...].T

    @pl.when(slab % 2 == 0)
    def _():
        step_ref[...] = link_ref[...]

    @pl.when(slab % 2 == 1)
    def _():
        step_ref[...] = dot(link_ref[...], before_ref[...]).astype(jnp.bfloat16)

    turned_step_ref[...] = step_ref[...].T
    size = green_ref.shape[0]
    stack_ref[:size] = green_ref[:, :size]
    stack_ref[size:] = green_ref[:, size:]
    first_ref[...] = adjoint(stack_ref[...], 1)
    second_ref[...] = adjoint(stack_ref[...], -1)

    @pl.when(slab // 2 == pair)
    def _():
        far_stack_ref[...] = dot(stack_ref[...], step_ref[...]).astype(jnp.bfloat16)
        far_first_ref[...] = adjoint(far_stack_ref[...], 1)
        far_second_ref[...] = adjoint(far_stack_ref[...], -1)
        quarter = size // 4
        columns = [far_stack_ref[:, i * quarter : (i + 1) * quarter] for i in range(4)]
        half_a_ref[...] = jnp.concatenate([columns[0], columns[2]], axis=1)
        half_b_ref[...] = jnp.concatenate([columns[1], columns[3]], axis=1)


def joined(refs):
    return jnp.concatenate([ref[...] for ref in refs], axis=0)


def carry_in(turn, link_ref, turned_ref, state, came, out_refs):
    rows = out_refs[0].shape[0]

    @pl.when(turn)
    def _():
        out = (unpacked(state).astype(jnp.float32) + moved(link_ref, turned_ref, unpacked(came))).astype(jnp.bfloat16)
        out = packed(out)
        for i, ref in enumerate(out_refs):
            ref[...] = out[i * rows : (i + 1) * rows]

    @pl.when(jnp.logical_not(turn))
    def _():
        for i, ref in enumerate(out_refs):
            ref[...] = state[i * rows : (i + 1) * rows]


def first_kernel(last_pair, link_ref, turned_ref, own_ref, came_ref, *out_refs):
    slab = lax.axis_index(SLAB)
    turn = jnp.logical_and(slab % 2 == 1, slab // 2 < last_pair)
    carry_in(turn, link_ref, turned_ref, own_ref[...], came_ref[...], out_refs)


def arrived(refs):
    near, far = refs[: len(refs) // 2], refs[len(refs) // 2 :]
    return jnp.where(lax.axis_index(SLAB) % 2 == 0, joined(near), joined(far))


def advance_kernel(pair, link_ref, turned_ref, *refs):
    parts = len(refs) // 4
    state, came, outs = refs[:parts], refs[parts : 3 * parts], refs[3 * parts :]
    carry_in(lax.axis_index(SLAB) // 2 == pair, link_ref, turned_ref, joined(state), arrived(came), outs)


def base_kernel(last_pair, link_ref, turned_ref, stack_ref, first_ref, second_ref, *refs):
    *state, came_re_ref, came_im_ref, out_ref, re_ref, im_ref = refs
    slab = lax.axis_index(SLAB)
    turn = jnp.logical_and(slab % 2 == 1, slab // 2 == last_pair)
    for parts, came_ref, ref in ((state[:2], came_re_ref, re_ref), (state[2:], came_im_ref, im_ref)):
        own = unpacked(joined(parts))

        @pl.when(turn)
        def _():
            ref[...] = (own.astype(jnp.float32) + moved(link_ref, turned_ref, unpacked(came_ref[...]))).astype(jnp.bfloat16)

        @pl.when(jnp.logical_not(turn))
        def _():
            ref[...] = own

    re, im = dot(stack_ref[...], re_ref[...]), dot(stack_ref[...], im_ref[...])
    size = re.shape[1]
    left_re = (re[:size] - im[size:]).astype(jnp.bfloat16)
    left_im = (im[:size] + re[size:]).astype(jnp.bfloat16)
    out_ref[...] = dot(left_re, first_ref[...]) + dot(left_im, second_ref[...])


def left_kernel(pair, matrix_ref, *refs):
    *came, out_ref = refs

    @pl.when(lax.axis_index(SLAB) // 2 == pair)
    def _():
        out_ref[...] = dot(matrix_ref[...], unpacked(arrived(came)))


def late_kernel(pair, far_first_ref, far_second_ref, half_ref, base_ref, re_ref, im_ref, *refs):
    *came, out_ref, left_re_ref, left_im_ref, result_ref, sems = refs
    size, width = result_ref.shape
    turn = lax.axis_index(SLAB) // 2 == pair
    cut = width // 256 * 128 if width % 128 == 0 else width // 2

    @pl.when(turn)
    def _():
        im = im_ref[...] + dot(half_ref[...], unpacked(arrived(came)))
        left_re_ref[...] = (re_ref[:size] - im[size:]).astype(jnp.bfloat16)
        left_im_ref[...] = (im[:size] + re_ref[size:]).astype(jnp.bfloat16)

    copies = []
    for n, block in enumerate((slice(0, cut), slice(cut, width))):

        @pl.when(turn)
        def _():
            late = dot(left_re_ref[...], far_first_ref[:, block]) + dot(left_im_ref[...], far_second_ref[:, block])
            result_ref[:, block] = (base_ref[:, block] + late).astype(jnp.bfloat16)

        @pl.when(jnp.logical_not(turn))
        def _():
            result_ref[:, block] = base_ref[:, block].astype(jnp.bfloat16)

        copy = pltpu.make_async_copy(result_ref.at[:, block], out_ref.at[:, block], sems.at[n])
        copy.start()
        copies.append(copy)
    for copy in copies:
        copy.wait()


def local(g_lesser, g_retarded, screened, coupling):
    devices = lax.axis_size(ENERGY)
    slabs = lax.axis_size(SLAB)
    chips = devices // 2
    me = lax.axis_index(ENERGY)
    chip, side = me // 2, me % 2

    lesser = g_lesser[0, 0]
    size, width = lesser.shape
    rows = size // chips
    inter = screened[:, 0]
    inter_other = swap_with(inter, 1)
    first = jnp.where(side == 0, inter, inter_other)
    second = jnp.where(side == 0, inter_other, inter)
    inter_rows = jnp.concatenate([first, second], axis=1)

    mine = [lax.dynamic_slice(lesser, (rows * (chip ^ j), 0), (rows, width)) for j in range(chips)]
    pieces = [mine[0]] + [swap_with(mine[j], 2 * j) for j in range(1, chips)]

    link = coupling[0]
    other_in_pair = {s: s ^ 1 for s in range(slabs)}
    link_before = swap_slabs(link, other_in_pair)

    pieces = pieces + [swap_with(x, 1) for x in pieces]
    sigma = convolve(chips, inter_rows, pieces)
    sigma, link_before = lax.optimization_barrier((sigma, link_before))
    own_re, own_im = gathered(sigma, [swap_with(sigma[j], 2 * j) for j in range(1, chips)])

    own_re, own_im, link_before = lax.optimization_barrier((own_re, own_im, link_before))
    square = (link.shape, jnp.bfloat16)
    tall, wide = ((2 * size, size), jnp.bfloat16), ((size, 2 * size), jnp.bfloat16)
    thin = ((2 * size, size // 2), jnp.bfloat16)
    last_pair = slabs // 2 - 1
    prepared = call(
        functools.partial(prepare_kernel, last_pair),
        [square, square, square, tall, wide, wide, tall, wide, wide, thin, thin],
        [link, link_before, g_retarded[0, 0]],
    )
    turned, step, turned_step, *base, far_stack, far_first, far_second, half_a, half_b = prepared
    came_re = swap_slabs(own_re, other_in_pair)
    came_im = swap_slabs(own_im, other_in_pair)
    part = ((size // 2, width), own_im.dtype)
    halves = [((size // 4, width), own_im.dtype)] * 2
    total = [((size, width), jnp.float32)]
    first = functools.partial(first_kernel, last_pair)
    re = call(first, halves, [link, turned, own_re, came_re])
    im = call(first, halves, [link, turned, own_im, came_im])

    for s in range(1, slabs - 1, 2):
        pair = (s + 1) // 2
        near, far = {s: s + 1, s + 1: s}, {s + 1: s + 2, s + 2: s + 1}
        near_re = [swap_slabs(x, near, 2) for x in re]
        near_im = [swap_slabs(x, near, 2) for x in im]
        if pair == last_pair:
            near_im[1], came_re, came_im = lax.optimization_barrier((near_im[1], came_re, came_im))
        far_re = [swap_slabs(x, far) for x in near_re]
        far_im = [swap_slabs(x, far) for x in near_im]
        if pair < last_pair:
            advance = functools.partial(advance_kernel, pair)
            re = call(advance, halves, [step, turned_step, *re, *near_re, *far_re])
            im = call(advance, halves, [step, turned_step, *im, *near_im, *far_im])
    total = [((size, width), jnp.float32)]
    given = [link, turned, *base, *re, *im, came_re, came_im]
    scratch = [pltpu.VMEM(link.shape, link.dtype)] * 2
    (out,) = call(functools.partial(base_kernel, last_pair), total, given, scratch)
    left = functools.partial(left_kernel, last_pair)
    products = [((2 * size, size), jnp.float32)]
    far_re[0], out = lax.optimization_barrier((far_re[0], out))
    (left_re,) = call(left, products, [far_stack, *near_re, *far_re])
    far_im[0], left_re = lax.optimization_barrier((far_im[0], left_re))
    (left_im,) = call(left, products, [half_a, near_im[0], far_im[0]])
    given = [far_first, far_second, half_b, out, left_re, left_im, near_im[1], far_im[1]]
    out = pl.pallas_call(
        functools.partial(late_kernel, last_pair),
        out_shape=jax.ShapeDtypeStruct((size, width), jnp.bfloat16),
        in_specs=[WHOLE] * len(given),
        out_specs=pl.BlockSpec(memory_space=pl.ANY),
        scratch_shapes=[
            pltpu.VMEM((size, size), jnp.bfloat16),
            pltpu.VMEM((size, size), jnp.bfloat16),
            pltpu.VMEM((size, width), jnp.bfloat16),
            pltpu.SemaphoreType.DMA((2,)),
        ],
        compiler_params=pltpu.CompilerParams(vmem_limit_bytes=10 << 20),
    )(*in_vmem(*given))
    return out[None, None]


def solution(mesh):
    placed = (
        P(ENERGY, SLAB, None, None),
        P(ENERGY, SLAB, None, None),
        P(None, SLAB, ENERGY, None),
        P(SLAB, None, None),
    )
    return jax.shard_map(
        local,
        mesh=mesh,
        in_specs=placed,
        out_specs=P(ENERGY, SLAB, None, None),
        check_vma=False,
    )
```

```python
import functools

import jax
import jax.numpy as jnp
from jax import lax
from jax.experimental import pallas as pl
from jax.experimental.pallas import tpu as pltpu
from jax.sharding import PartitionSpec as P

ENERGY = "energy"
SLAB = "slab"
WHOLE = pl.BlockSpec(memory_space=pltpu.VMEM)


def in_vmem(*arrays):
    return [pltpu.with_memory_space_constraint(x, pltpu.VMEM) for x in arrays]


def swap_with(array, mask):
    devices = lax.axis_size(ENERGY)
    return lax.ppermute(array, ENERGY, [(i, i ^ mask) for i in range(devices)])


def swap_slabs(array, slab_to, idle=1):
    devices, slabs = lax.axis_size(ENERGY), lax.axis_size(SLAB)
    pairs = []
    for e in range(devices):
        for s in range(slabs):
            to = (e, slab_to[s]) if s in slab_to else (e ^ idle, s)
            pairs.append((e * slabs + s, to[0] * slabs + to[1]))
    return lax.ppermute(array, (ENERGY, SLAB), pairs)


def call(kernel, outs, given, scratch=()):
    outs = [pltpu.VMEM(shape, dtype) for shape, dtype in outs]
    return pl.pallas_call(
        kernel,
        out_shape=outs,
        in_specs=[WHOLE] * len(given),
        out_specs=[WHOLE] * len(outs),
        scratch_shapes=list(scratch),
        compiler_params=pltpu.CompilerParams(vmem_limit_bytes=10 << 20),
    )(*in_vmem(*given))


def conv_kernel(chips, inter_ref, *refs):
    pieces = refs[: 2 * chips]
    out_ref, a_ref, b_ref, w_ref, v_ref, sum_ref = refs[2 * chips :]
    me = lax.axis_index(ENERGY)
    chip, side = me // 2, me % 2
    rows, width = inter_ref.shape[1:]
    half = width // 2
    left = lax.broadcasted_iota(jnp.int32, (rows, width), 1) < half

    def swapped(x):
        return jnp.concatenate([x[:, half:], x[:, :half]], axis=1)

    @pl.when(side == 0)
    def _():
        a_ref[0] = jnp.zeros((rows, width), jnp.float32)
        b_ref[0] = jnp.zeros((rows, width), jnp.float32)

    for other in range(2):
        for j in range(chips):
            x = pieces[other * chips + j][...].astype(jnp.float32)
            y = swapped(x)
            slot = 2 * (chip ^ j) + (side ^ other) + 1 - side
            a_ref[slot] = jnp.where(left, x, y)
            b_ref[slot] = jnp.where(left, y, x)
    for m in range(2 * chips):
        x = inter_ref[m].astype(jnp.float32)
        y = swapped(x)
        w_ref[m] = x
        v_ref[m] = jnp.where(left, -y, y)

    step = 8 if rows % 8 == 0 else rows
    lanes = 128 if width % 128 == 0 else width

    def tile(t, carry):
        here = pl.ds(pl.multiple_of(t * step, step), step)
        for c in range(0, width, lanes):
            at = pl.ds(c, lanes)
            for j in range(chips):
                total = None
                for m in range(2 * j + 2):
                    s = 2 * j + 1 - m
                    term = a_ref[s, here, at] * v_ref[m, here, at] - b_ref[s, here, at] * w_ref[m, here, at]
                    total = term if total is None else total + term
                sum_ref[chip ^ j, here, at] = total
        return carry

    lax.fori_loop(0, rows // step, tile, 0)
    out_ref[...] = sum_ref[...].astype(jnp.bfloat16)


def convolve(chips, inter, pieces):
    count, rows, width = inter.shape
    block = lambda n: pltpu.VMEM((n, rows, width), jnp.float32)
    return pl.pallas_call(
        functools.partial(conv_kernel, chips),
        out_shape=pltpu.VMEM((chips, rows, width), jnp.bfloat16),
        in_specs=[WHOLE] * (1 + 2 * chips),
        out_specs=WHOLE,
        scratch_shapes=[block(count + 1), block(count + 1), block(count), block(count), block(chips)],
        compiler_params=pltpu.CompilerParams(vmem_limit_bytes=16 << 20),
        cost_estimate=pl.CostEstimate(flops=count * count * rows * width * 4, bytes_accessed=0, transcendentals=0),
    )(*in_vmem(inter, *pieces))


def dot(a, b):
    return jnp.dot(a, b, preferred_element_type=jnp.float32)


def packed(x):
    half = x.shape[0] // 2
    return jnp.concatenate([x[:half], x[half:]], axis=1)


def unpacked(x):
    size = x.shape[1] // 2
    return jnp.concatenate([x[:, :size], x[:, size:]], axis=0)


def moved(link_ref, turned_ref, x):
    return dot(dot(link_ref[...], x).astype(jnp.bfloat16), turned_ref[...])


def gather_kernel(*refs):
    chip = lax.axis_index(ENERGY) // 2
    first_ref, *others, re_ref, im_ref, all_ref = refs
    all_ref[chip] = first_ref[0]
    for j, ref in enumerate(others):
        all_ref[chip ^ (j + 1)] = ref[...]
    chips, rows, width = all_ref.shape
    whole = all_ref[...].reshape(chips * rows, width)
    re_ref[...] = packed(whole[:, : width // 2])
    im_ref[...] = packed(whole[:, width // 2 :])


def gathered(own, pieces):
    chips, rows, width = own.shape
    part = ((chips * rows // 2, width), jnp.bfloat16)
    return call(gather_kernel, [part, part], [own, *pieces], [pltpu.VMEM(own.shape, own.dtype)])


def adjoint(stack, sign):
    size = stack.shape[1]
    re, im = stack[:size], stack[size:]
    return jnp.concatenate([re, -im] if sign > 0 else [im, re], axis=0).T


def prepare_kernel(pair, link_ref, before_ref, green_ref, turned_ref, step_ref, turned_step_ref, *refs):
    stack_ref, first_ref, second_ref, far_stack_ref, far_first_ref, far_second_ref, half_a_ref, half_b_ref = refs
    slab = lax.axis_index(SLAB)
    turned_ref[...] = link_ref[...].T

    @pl.when(slab % 2 == 0)
    def _():
        step_ref[...] = link_ref[...]

    @pl.when(slab % 2 == 1)
    def _():
        step_ref[...] = dot(link_ref[...], before_ref[...]).astype(jnp.bfloat16)

    turned_step_ref[...] = step_ref[...].T
    size = green_ref.shape[0]
    stack_ref[:size] = green_ref[:, :size]
    stack_ref[size:] = green_ref[:, size:]
    first_ref[...] = adjoint(stack_ref[...], 1)
    second_ref[...] = adjoint(stack_ref[...], -1)

    @pl.when(slab // 2 == pair)
    def _():
        far_stack_ref[...] = dot(stack_ref[...], step_ref[...]).astype(jnp.bfloat16)
        far_first_ref[...] = adjoint(far_stack_ref[...], 1)
        far_second_ref[...] = adjoint(far_stack_ref[...], -1)
        quarter = size // 4
        columns = [far_stack_ref[:, i * quarter : (i + 1) * quarter] for i in range(4)]
        half_a_ref[...] = jnp.concatenate([columns[0], columns[2]], axis=1)
        half_b_ref[...] = jnp.concatenate([columns[1], columns[3]], axis=1)


def joined(refs):
    return jnp.concatenate([ref[...] for ref in refs], axis=0)


def carry_in(turn, link_ref, turned_ref, state, came, out_refs):
    rows = out_refs[0].shape[0]

    @pl.when(turn)
    def _():
        out = (unpacked(state).astype(jnp.float32) + moved(link_ref, turned_ref, unpacked(came))).astype(jnp.bfloat16)
        out = packed(out)
        for i, ref in enumerate(out_refs):
            ref[...] = out[i * rows : (i + 1) * rows]

    @pl.when(jnp.logical_not(turn))
    def _():
        for i, ref in enumerate(out_refs):
            ref[...] = state[i * rows : (i + 1) * rows]


def first_kernel(last_pair, link_ref, turned_ref, own_ref, came_ref, *out_refs):
    slab = lax.axis_index(SLAB)
    turn = jnp.logical_and(slab % 2 == 1, slab // 2 < last_pair)
    carry_in(turn, link_ref, turned_ref, own_ref[...], came_ref[...], out_refs)


def arrived(refs):
    near, far = refs[: len(refs) // 2], refs[len(refs) // 2 :]
    return jnp.where(lax.axis_index(SLAB) % 2 == 0, joined(near), joined(far))


def advance_kernel(pair, link_ref, turned_ref, *refs):
    parts = len(refs) // 4
    state, came, outs = refs[:parts], refs[parts : 3 * parts], refs[3 * parts :]
    carry_in(lax.axis_index(SLAB) // 2 == pair, link_ref, turned_ref, joined(state), arrived(came), outs)


def base_kernel(last_pair, link_ref, turned_ref, stack_ref, first_ref, second_ref, *refs):
    *state, came_re_ref, came_im_ref, out_ref, re_ref, im_ref = refs
    slab = lax.axis_index(SLAB)
    turn = jnp.logical_and(slab % 2 == 1, slab // 2 == last_pair)
    for parts, came_ref, ref in ((state[:2], came_re_ref, re_ref), (state[2:], came_im_ref, im_ref)):
        own = unpacked(joined(parts))

        @pl.when(turn)
        def _():
            ref[...] = (own.astype(jnp.float32) + moved(link_ref, turned_ref, unpacked(came_ref[...]))).astype(jnp.bfloat16)

        @pl.when(jnp.logical_not(turn))
        def _():
            ref[...] = own

    re, im = dot(stack_ref[...], re_ref[...]), dot(stack_ref[...], im_ref[...])
    size = re.shape[1]
    left_re = (re[:size] - im[size:]).astype(jnp.bfloat16)
    left_im = (im[:size] + re[size:]).astype(jnp.bfloat16)
    out_ref[...] = dot(left_re, first_ref[...]) + dot(left_im, second_ref[...])


def left_kernel(pair, matrix_ref, *refs):
    *came, out_ref = refs

    @pl.when(lax.axis_index(SLAB) // 2 == pair)
    def _():
        out_ref[...] = dot(matrix_ref[...], unpacked(arrived(came)))


def late_kernel(pair, far_first_ref, far_second_ref, half_ref, base_ref, re_ref, im_ref, *refs):
    *came, out_ref, left_re_ref, left_im_ref, result_ref, sems = refs
    size, width = result_ref.shape
    turn = lax.axis_index(SLAB) // 2 == pair
    cut = width // 256 * 256 if width > 256 else width // 2

    @pl.when(turn)
    def _():
        im = im_ref[...] + dot(half_ref[...], unpacked(arrived(came)))
        left_re_ref[...] = (re_ref[:size] - im[size:]).astype(jnp.bfloat16)
        left_im_ref[...] = (im[:size] + re_ref[size:]).astype(jnp.bfloat16)

    copies = []
    for n, block in enumerate((slice(0, cut), slice(cut, width))):

        @pl.when(turn)
        def _():
            late = dot(left_re_ref[...], far_first_ref[:, block]) + dot(left_im_ref[...], far_second_ref[:, block])
            result_ref[:, block] = (base_ref[:, block] + late).astype(jnp.bfloat16)

        @pl.when(jnp.logical_not(turn))
        def _():
            result_ref[:, block] = base_ref[:, block].astype(jnp.bfloat16)

        copy = pltpu.make_async_copy(result_ref.at[:, block], out_ref.at[:, block], sems.at[n])
        copy.start()
        copies.append(copy)
    for copy in copies:
        copy.wait()


def local(g_lesser, g_retarded, screened, coupling):
    devices = lax.axis_size(ENERGY)
    slabs = lax.axis_size(SLAB)
    chips = devices // 2
    me = lax.axis_index(ENERGY)
    chip, side = me // 2, me % 2

    lesser = g_lesser[0, 0]
    size, width = lesser.shape
    rows = size // chips
    inter = screened[:, 0]
    inter_other = swap_with(inter, 1)
    first = jnp.where(side == 0, inter, inter_other)
    second = jnp.where(side == 0, inter_other, inter)
    inter_rows = jnp.concatenate([first, second], axis=1)

    mine = [lax.dynamic_slice(lesser, (rows * (chip ^ j), 0), (rows, width)) for j in range(chips)]
    pieces = [mine[0]] + [swap_with(mine[j], 2 * j) for j in range(1, chips)]

    link = coupling[0]
    other_in_pair = {s: s ^ 1 for s in range(slabs)}
    link_before = swap_slabs(link, other_in_pair)

    pieces = pieces + [swap_with(x, 1) for x in pieces]
    sigma = convolve(chips, inter_rows, pieces)
    sigma, link_before = lax.optimization_barrier((sigma, link_before))
    own_re, own_im = gathered(sigma, [swap_with(sigma[j], 2 * j) for j in range(1, chips)])

    own_re, own_im, link_before = lax.optimization_barrier((own_re, own_im, link_before))
    square = (link.shape, jnp.bfloat16)
    tall, wide = ((2 * size, size), jnp.bfloat16), ((size, 2 * size), jnp.bfloat16)
    thin = ((2 * size, size // 2), jnp.bfloat16)
    last_pair = slabs // 2 - 1
    prepared = call(
        functools.partial(prepare_kernel, last_pair),
        [square, square, square, tall, wide, wide, tall, wide, wide, thin, thin],
        [link, link_before, g_retarded[0, 0]],
    )
    turned, step, turned_step, *base, far_stack, far_first, far_second, half_a, half_b = prepared
    came_re = swap_slabs(own_re, other_in_pair)
    came_im = swap_slabs(own_im, other_in_pair)
    part = ((size // 2, width), own_im.dtype)
    halves = [((size // 4, width), own_im.dtype)] * 2
    total = [((size, width), jnp.float32)]
    first = functools.partial(first_kernel, last_pair)
    re = call(first, halves, [link, turned, own_re, came_re])
    im = call(first, halves, [link, turned, own_im, came_im])

    for s in range(1, slabs - 1, 2):
        pair = (s + 1) // 2
        near, far = {s: s + 1, s + 1: s}, {s + 1: s + 2, s + 2: s + 1}
        near_re = [swap_slabs(x, near, 2) for x in re]
        near_im = [swap_slabs(x, near, 2) for x in im]
        if pair == last_pair:
            near_im[1], came_re, came_im = lax.optimization_barrier((near_im[1], came_re, came_im))
        far_re = [swap_slabs(x, far) for x in near_re]
        far_im = [swap_slabs(x, far) for x in near_im]
        if pair < last_pair:
            advance = functools.partial(advance_kernel, pair)
            re = call(advance, halves, [step, turned_step, *re, *near_re, *far_re])
            im = call(advance, halves, [step, turned_step, *im, *near_im, *far_im])
    total = [((size, width), jnp.float32)]
    given = [link, turned, *base, *re, *im, came_re, came_im]
    scratch = [pltpu.VMEM(link.shape, link.dtype)] * 2
    (out,) = call(functools.partial(base_kernel, last_pair), total, given, scratch)
    left = functools.partial(left_kernel, last_pair)
    products = [((2 * size, size), jnp.float32)]
    far_re[0], out = lax.optimization_barrier((far_re[0], out))
    (left_re,) = call(left, products, [far_stack, *near_re, *far_re])
    far_im[0], left_re = lax.optimization_barrier((far_im[0], left_re))
    (left_im,) = call(left, products, [half_a, near_im[0], far_im[0]])
    given = [far_first, far_second, half_b, out, left_re, left_im, near_im[1], far_im[1]]
    out = pl.pallas_call(
        functools.partial(late_kernel, last_pair),
        out_shape=jax.ShapeDtypeStruct((size, width), jnp.bfloat16),
        in_specs=[WHOLE] * len(given),
        out_specs=pl.BlockSpec(memory_space=pl.ANY),
        scratch_shapes=[
            pltpu.VMEM((size, size), jnp.bfloat16),
            pltpu.VMEM((size, size), jnp.bfloat16),
            pltpu.VMEM((size, width), jnp.bfloat16),
            pltpu.SemaphoreType.DMA((2,)),
        ],
        compiler_params=pltpu.CompilerParams(vmem_limit_bytes=10 << 20),
    )(*in_vmem(*given))
    return out[None, None]


def solution(mesh):
    placed = (
        P(ENERGY, SLAB, None, None),
        P(ENERGY, SLAB, None, None),
        P(None, SLAB, ENERGY, None),
        P(SLAB, None, None),
    )
    return jax.shard_map(
        local,
        mesh=mesh,
        in_specs=placed,
        out_specs=P(ENERGY, SLAB, None, None),
        check_vma=False,
    )
```

```python
import functools

import jax
import jax.numpy as jnp
from jax import lax
from jax.experimental import pallas as pl
from jax.experimental.pallas import tpu as pltpu
from jax.sharding import PartitionSpec as P

ENERGY = "energy"
SLAB = "slab"
WHOLE = pl.BlockSpec(memory_space=pltpu.VMEM)


def in_vmem(*arrays):
    return [pltpu.with_memory_space_constraint(x, pltpu.VMEM) for x in arrays]


def swap_with(array, mask):
    devices = lax.axis_size(ENERGY)
    return lax.ppermute(array, ENERGY, [(i, i ^ mask) for i in range(devices)])


def swap_slabs(array, slab_to, idle=1):
    devices, slabs = lax.axis_size(ENERGY), lax.axis_size(SLAB)
    pairs = []
    for e in range(devices):
        for s in range(slabs):
            to = (e, slab_to[s]) if s in slab_to else (e ^ idle, s)
            pairs.append((e * slabs + s, to[0] * slabs + to[1]))
    return lax.ppermute(array, (ENERGY, SLAB), pairs)


def call(kernel, outs, given, scratch=()):
    outs = [pltpu.VMEM(shape, dtype) for shape, dtype in outs]
    return pl.pallas_call(
        kernel,
        out_shape=outs,
        in_specs=[WHOLE] * len(given),
        out_specs=[WHOLE] * len(outs),
        scratch_shapes=list(scratch),
        compiler_params=pltpu.CompilerParams(vmem_limit_bytes=10 << 20),
    )(*in_vmem(*given))


def spread_kernel(inter_ref, other_ref, w_ref, v_ref):
    side = lax.axis_index(ENERGY) % 2
    count, rows, width = inter_ref.shape
    left = lax.broadcasted_iota(jnp.int32, (2 * rows, width), 1) < width // 2
    for m in range(count):
        own, other = inter_ref[m].astype(jnp.float32), other_ref[m].astype(jnp.float32)
        x = jnp.concatenate([jnp.where(side == 0, own, other), jnp.where(side == 0, other, own)], axis=0)
        y = jnp.concatenate([x[:, width // 2 :], x[:, : width // 2]], axis=1)
        w_ref[m] = x
        v_ref[m] = jnp.where(left, -y, y)


def conv_kernel(chips, w_ref, v_ref, *refs):
    pieces = refs[: 2 * chips]
    out_ref, a_ref, b_ref, sum_ref = refs[2 * chips :]
    me = lax.axis_index(ENERGY)
    chip, side = me // 2, me % 2
    rows, width = w_ref.shape[1:]
    half = width // 2
    left = lax.broadcasted_iota(jnp.int32, (rows, width), 1) < half

    def swapped(x):
        return jnp.concatenate([x[:, half:], x[:, :half]], axis=1)

    @pl.when(side == 0)
    def _():
        a_ref[0] = jnp.zeros((rows, width), jnp.float32)
        b_ref[0] = jnp.zeros((rows, width), jnp.float32)

    for other in range(2):
        for j in range(chips):
            x = pieces[other * chips + j][...].astype(jnp.float32)
            y = swapped(x)
            slot = 2 * (chip ^ j) + (side ^ other) + 1 - side
            a_ref[slot] = jnp.where(left, x, y)
            b_ref[slot] = jnp.where(left, y, x)
    step = 8 if rows % 8 == 0 else rows
    lanes = 128 if width % 128 == 0 else width

    def tile(t, carry):
        here = pl.ds(pl.multiple_of(t * step, step), step)
        for c in range(0, width, lanes):
            at = pl.ds(c, lanes)
            for j in range(chips):
                total = None
                for m in range(2 * j + 2):
                    s = 2 * j + 1 - m
                    term = a_ref[s, here, at] * v_ref[m, here, at] - b_ref[s, here, at] * w_ref[m, here, at]
                    total = term if total is None else total + term
                sum_ref[chip ^ j, here, at] = total
        return carry

    lax.fori_loop(0, rows // step, tile, 0)
    out_ref[...] = sum_ref[...].astype(jnp.bfloat16)


def convolve(chips, inter, pieces):
    count, rows, width = inter[0].shape
    block = lambda n: pltpu.VMEM((n, rows, width), jnp.float32)
    return pl.pallas_call(
        functools.partial(conv_kernel, chips),
        out_shape=pltpu.VMEM((chips, rows, width), jnp.bfloat16),
        in_specs=[WHOLE] * (2 + 2 * chips),
        out_specs=WHOLE,
        scratch_shapes=[block(count + 1), block(count + 1), block(chips)],
        compiler_params=pltpu.CompilerParams(vmem_limit_bytes=16 << 20),
        cost_estimate=pl.CostEstimate(flops=count * count * rows * width * 4, bytes_accessed=0, transcendentals=0),
    )(*in_vmem(*inter, *pieces))


def dot(a, b):
    return jnp.dot(a, b, preferred_element_type=jnp.float32)


def packed(x):
    half = x.shape[0] // 2
    return jnp.concatenate([x[:half], x[half:]], axis=1)


def unpacked(x):
    size = x.shape[1] // 2
    return jnp.concatenate([x[:, :size], x[:, size:]], axis=0)


def moved(link_ref, turned_ref, x):
    return dot(dot(link_ref[...], x).astype(jnp.bfloat16), turned_ref[...])


def gather_kernel(*refs):
    chip = lax.axis_index(ENERGY) // 2
    first_ref, *others, re_ref, im_ref, all_ref = refs
    all_ref[chip] = first_ref[0]
    for j, ref in enumerate(others):
        all_ref[chip ^ (j + 1)] = ref[...]
    chips, rows, width = all_ref.shape
    whole = all_ref[...].reshape(chips * rows, width)
    re_ref[...] = packed(whole[:, : width // 2])
    im_ref[...] = packed(whole[:, width // 2 :])


def gathered(own, pieces):
    chips, rows, width = own.shape
    part = ((chips * rows // 2, width), jnp.bfloat16)
    return call(gather_kernel, [part, part], [own, *pieces], [pltpu.VMEM(own.shape, own.dtype)])


def adjoint(stack, sign):
    size = stack.shape[1]
    re, im = stack[:size], stack[size:]
    return jnp.concatenate([re, -im] if sign > 0 else [im, re], axis=0).T


def prepare_kernel(pair, link_ref, before_ref, green_ref, turned_ref, step_ref, turned_step_ref, *refs):
    stack_ref, first_ref, second_ref, far_stack_ref, far_first_ref, far_second_ref, half_a_ref, half_b_ref = refs
    slab = lax.axis_index(SLAB)
    turned_ref[...] = link_ref[...].T

    @pl.when(slab % 2 == 0)
    def _():
        step_ref[...] = link_ref[...]

    @pl.when(slab % 2 == 1)
    def _():
        step_ref[...] = dot(link_ref[...], before_ref[...]).astype(jnp.bfloat16)

    turned_step_ref[...] = step_ref[...].T
    size = green_ref.shape[0]
    stack_ref[:size] = green_ref[:, :size]
    stack_ref[size:] = green_ref[:, size:]
    first_ref[...] = adjoint(stack_ref[...], 1)
    second_ref[...] = adjoint(stack_ref[...], -1)

    @pl.when(slab // 2 == pair)
    def _():
        far_stack_ref[...] = dot(stack_ref[...], step_ref[...]).astype(jnp.bfloat16)
        far_first_ref[...] = adjoint(far_stack_ref[...], 1)
        far_second_ref[...] = adjoint(far_stack_ref[...], -1)
        quarter = size // 4
        columns = [far_stack_ref[:, i * quarter : (i + 1) * quarter] for i in range(4)]
        half_a_ref[...] = jnp.concatenate([columns[0], columns[2]], axis=1)
        half_b_ref[...] = jnp.concatenate([columns[1], columns[3]], axis=1)


def joined(refs):
    return jnp.concatenate([ref[...] for ref in refs], axis=0)


def carry_in(turn, link_ref, turned_ref, state, came, out_refs):
    rows = out_refs[0].shape[0]

    @pl.when(turn)
    def _():
        out = (unpacked(state).astype(jnp.float32) + moved(link_ref, turned_ref, unpacked(came))).astype(jnp.bfloat16)
        out = packed(out)
        for i, ref in enumerate(out_refs):
            ref[...] = out[i * rows : (i + 1) * rows]

    @pl.when(jnp.logical_not(turn))
    def _():
        for i, ref in enumerate(out_refs):
            ref[...] = state[i * rows : (i + 1) * rows]


def first_kernel(last_pair, link_ref, turned_ref, own_ref, came_ref, *out_refs):
    slab = lax.axis_index(SLAB)
    turn = jnp.logical_and(slab % 2 == 1, slab // 2 < last_pair)
    carry_in(turn, link_ref, turned_ref, own_ref[...], came_ref[...], out_refs)


def arrived(refs):
    near, far = refs[: len(refs) // 2], refs[len(refs) // 2 :]
    return jnp.where(lax.axis_index(SLAB) % 2 == 0, joined(near), joined(far))


def advance_kernel(pair, link_ref, turned_ref, *refs):
    parts = len(refs) // 4
    state, came, outs = refs[:parts], refs[parts : 3 * parts], refs[3 * parts :]
    carry_in(lax.axis_index(SLAB) // 2 == pair, link_ref, turned_ref, joined(state), arrived(came), outs)


def base_kernel(last_pair, link_ref, turned_ref, stack_ref, first_ref, second_ref, *refs):
    *state, came_re_ref, came_im_ref, out_ref, re_ref, im_ref = refs
    slab = lax.axis_index(SLAB)
    turn = jnp.logical_and(slab % 2 == 1, slab // 2 == last_pair)
    for parts, came_ref, ref in ((state[:2], came_re_ref, re_ref), (state[2:], came_im_ref, im_ref)):
        own = unpacked(joined(parts))

        @pl.when(turn)
        def _():
            ref[...] = (own.astype(jnp.float32) + moved(link_ref, turned_ref, unpacked(came_ref[...]))).astype(jnp.bfloat16)

        @pl.when(jnp.logical_not(turn))
        def _():
            ref[...] = own

    re, im = dot(stack_ref[...], re_ref[...]), dot(stack_ref[...], im_ref[...])
    size = re.shape[1]
    left_re = (re[:size] - im[size:]).astype(jnp.bfloat16)
    left_im = (im[:size] + re[size:]).astype(jnp.bfloat16)
    out_ref[...] = dot(left_re, first_ref[...]) + dot(left_im, second_ref[...])


def left_kernel(pair, matrix_ref, *refs):
    *came, out_ref = refs

    @pl.when(lax.axis_index(SLAB) // 2 == pair)
    def _():
        out_ref[...] = dot(matrix_ref[...], unpacked(arrived(came)))


def late_kernel(pair, far_first_ref, far_second_ref, half_ref, base_ref, re_ref, im_ref, *refs):
    *came, out_ref, left_re_ref, left_im_ref, result_ref, sems = refs
    size, width = result_ref.shape
    turn = lax.axis_index(SLAB) // 2 == pair
    cut = width // 256 * 256 if width > 256 else width // 2

    @pl.when(turn)
    def _():
        im = im_ref[...] + dot(half_ref[...], unpacked(arrived(came)))
        left_re_ref[...] = (re_ref[:size] - im[size:]).astype(jnp.bfloat16)
        left_im_ref[...] = (im[:size] + re_ref[size:]).astype(jnp.bfloat16)

    copies = []
    for n, block in enumerate((slice(0, cut), slice(cut, width))):

        @pl.when(turn)
        def _():
            late = dot(left_re_ref[...], far_first_ref[:, block]) + dot(left_im_ref[...], far_second_ref[:, block])
            result_ref[:, block] = (base_ref[:, block] + late).astype(jnp.bfloat16)

        @pl.when(jnp.logical_not(turn))
        def _():
            result_ref[:, block] = base_ref[:, block].astype(jnp.bfloat16)

        copy = pltpu.make_async_copy(result_ref.at[:, block], out_ref.at[:, block], sems.at[n])
        copy.start()
        copies.append(copy)
    for copy in copies:
        copy.wait()


def local(g_lesser, g_retarded, screened, coupling):
    devices = lax.axis_size(ENERGY)
    slabs = lax.axis_size(SLAB)
    chips = devices // 2
    me = lax.axis_index(ENERGY)
    chip, side = me // 2, me % 2

    lesser = g_lesser[0, 0]
    size, width = lesser.shape
    rows = size // chips
    inter = screened[:, 0]
    inter_other = swap_with(inter, 1)
    spread = call(spread_kernel, [((devices, rows, width), jnp.float32)] * 2, [inter, inter_other])

    mine = [lax.dynamic_slice(lesser, (rows * (chip ^ j), 0), (rows, width)) for j in range(chips)]
    pieces = [mine[0]] + [swap_with(mine[j], 2 * j) for j in range(1, chips)]

    link = coupling[0]
    other_in_pair = {s: s ^ 1 for s in range(slabs)}
    link, spread = lax.optimization_barrier((link, spread))
    link_before = swap_slabs(link, other_in_pair)

    pieces = pieces + [swap_with(x, 1) for x in pieces]
    sigma = convolve(chips, spread, pieces)
    sigma, link_before = lax.optimization_barrier((sigma, link_before))
    own_re, own_im = gathered(sigma, [swap_with(sigma[j], 2 * j) for j in range(1, chips)])

    own_re, own_im, link_before = lax.optimization_barrier((own_re, own_im, link_before))
    square = (link.shape, jnp.bfloat16)
    tall, wide = ((2 * size, size), jnp.bfloat16), ((size, 2 * size), jnp.bfloat16)
    thin = ((2 * size, size // 2), jnp.bfloat16)
    last_pair = slabs // 2 - 1
    prepared = call(
        functools.partial(prepare_kernel, last_pair),
        [square, square, square, tall, wide, wide, tall, wide, wide, thin, thin],
        [link, link_before, g_retarded[0, 0]],
    )
    turned, step, turned_step, *base, far_stack, far_first, far_second, half_a, half_b = prepared
    came_re = swap_slabs(own_re, other_in_pair)
    came_im = swap_slabs(own_im, other_in_pair)
    part = ((size // 2, width), own_im.dtype)
    halves = [((size // 4, width), own_im.dtype)] * 2
    total = [((size, width), jnp.float32)]
    first = functools.partial(first_kernel, last_pair)
    re = call(first, halves, [link, turned, own_re, came_re])
    im = call(first, halves, [link, turned, own_im, came_im])

    for s in range(1, slabs - 1, 2):
        pair = (s + 1) // 2
        near, far = {s: s + 1, s + 1: s}, {s + 1: s + 2, s + 2: s + 1}
        near_re = [swap_slabs(x, near, 2) for x in re]
        near_im = [swap_slabs(x, near, 2) for x in im]
        if pair == last_pair:
            near_im[1], came_re, came_im = lax.optimization_barrier((near_im[1], came_re, came_im))
        far_re = [swap_slabs(x, far) for x in near_re]
        far_im = [swap_slabs(x, far) for x in near_im]
        if pair < last_pair:
            advance = functools.partial(advance_kernel, pair)
            re = call(advance, halves, [step, turned_step, *re, *near_re, *far_re])
            im = call(advance, halves, [step, turned_step, *im, *near_im, *far_im])
    total = [((size, width), jnp.float32)]
    given = [link, turned, *base, *re, *im, came_re, came_im]
    scratch = [pltpu.VMEM(link.shape, link.dtype)] * 2
    (out,) = call(functools.partial(base_kernel, last_pair), total, given, scratch)
    left = functools.partial(left_kernel, last_pair)
    products = [((2 * size, size), jnp.float32)]
    far_re[0], out = lax.optimization_barrier((far_re[0], out))
    (left_re,) = call(left, products, [far_stack, *near_re, *far_re])
    far_im[0], left_re = lax.optimization_barrier((far_im[0], left_re))
    (left_im,) = call(left, products, [half_a, near_im[0], far_im[0]])
    given = [far_first, far_second, half_b, out, left_re, left_im, near_im[1], far_im[1]]
    out = pl.pallas_call(
        functools.partial(late_kernel, last_pair),
        out_shape=jax.ShapeDtypeStruct((size, width), jnp.bfloat16),
        in_specs=[WHOLE] * len(given),
        out_specs=pl.BlockSpec(memory_space=pl.ANY),
        scratch_shapes=[
            pltpu.VMEM((size, size), jnp.bfloat16),
            pltpu.VMEM((size, size), jnp.bfloat16),
            pltpu.VMEM((size, width), jnp.bfloat16),
            pltpu.SemaphoreType.DMA((2,)),
        ],
        compiler_params=pltpu.CompilerParams(vmem_limit_bytes=10 << 20),
    )(*in_vmem(*given))
    return out[None, None]


def solution(mesh):
    placed = (
        P(ENERGY, SLAB, None, None),
        P(ENERGY, SLAB, None, None),
        P(None, SLAB, ENERGY, None),
        P(SLAB, None, None),
    )
    return jax.shard_map(
        local,
        mesh=mesh,
        in_specs=placed,
        out_specs=P(ENERGY, SLAB, None, None),
        check_vma=False,
    )
```

```python
import functools

import jax
import jax.numpy as jnp
from jax import lax
from jax.experimental import pallas as pl
from jax.experimental.pallas import tpu as pltpu
from jax.sharding import PartitionSpec as P

ENERGY = "energy"
SLAB = "slab"
WHOLE = pl.BlockSpec(memory_space=pltpu.VMEM)


def in_vmem(*arrays):
    return [pltpu.with_memory_space_constraint(x, pltpu.VMEM) for x in arrays]


def in_order(chips):
    return [0] + sorted(range(1, chips), key=lambda j: (j & (j - 1) != 0, -j))


def swap_with(array, mask):
    devices = lax.axis_size(ENERGY)
    return lax.ppermute(array, ENERGY, [(i, i ^ mask) for i in range(devices)])


def swap_slabs(array, slab_to, idle=1):
    devices, slabs = lax.axis_size(ENERGY), lax.axis_size(SLAB)
    pairs = []
    for e in range(devices):
        for s in range(slabs):
            to = (e, slab_to[s]) if s in slab_to else (e ^ idle, s)
            pairs.append((e * slabs + s, to[0] * slabs + to[1]))
    return lax.ppermute(array, (ENERGY, SLAB), pairs)


def call(kernel, outs, given, scratch=()):
    outs = [pltpu.VMEM(shape, dtype) for shape, dtype in outs]
    return pl.pallas_call(
        kernel,
        out_shape=outs,
        in_specs=[WHOLE] * len(given),
        out_specs=[WHOLE] * len(outs),
        scratch_shapes=list(scratch),
        compiler_params=pltpu.CompilerParams(vmem_limit_bytes=10 << 20),
    )(*in_vmem(*given))


def spread_kernel(inter_ref, other_ref, w_ref, v_ref):
    side = lax.axis_index(ENERGY) % 2
    count, rows, width = inter_ref.shape
    left = lax.broadcasted_iota(jnp.int32, (2 * rows, width), 1) < width // 2
    for m in range(count):
        own, other = inter_ref[m].astype(jnp.float32), other_ref[m].astype(jnp.float32)
        x = jnp.concatenate([jnp.where(side == 0, own, other), jnp.where(side == 0, other, own)], axis=0)
        y = jnp.concatenate([x[:, width // 2 :], x[:, : width // 2]], axis=1)
        w_ref[m] = x
        v_ref[m] = jnp.where(left, -y, y)


def conv_kernel(chips, w_ref, v_ref, *refs):
    pieces = refs[: 2 * chips]
    out_ref, a_ref, b_ref, sum_ref = refs[2 * chips :]
    me = lax.axis_index(ENERGY)
    chip, side = me // 2, me % 2
    rows, width = w_ref.shape[1:]
    half = width // 2
    left = lax.broadcasted_iota(jnp.int32, (rows, width), 1) < half

    def swapped(x):
        return jnp.concatenate([x[:, half:], x[:, :half]], axis=1)

    @pl.when(side == 0)
    def _():
        a_ref[0] = jnp.zeros((rows, width), jnp.float32)
        b_ref[0] = jnp.zeros((rows, width), jnp.float32)

    for other in range(2):
        for j in range(chips):
            x = pieces[other * chips + j][...].astype(jnp.float32)
            y = swapped(x)
            slot = 2 * (chip ^ j) + (side ^ other) + 1 - side
            a_ref[slot] = jnp.where(left, x, y)
            b_ref[slot] = jnp.where(left, y, x)
    step = 8 if rows % 8 == 0 else rows
    lanes = 128 if width % 128 == 0 else width

    def tile(t, carry):
        here = pl.ds(pl.multiple_of(t * step, step), step)
        for c in range(0, width, lanes):
            at = pl.ds(c, lanes)
            for j in range(chips):
                total = None
                for m in range(2 * j + 2):
                    s = 2 * j + 1 - m
                    term = a_ref[s, here, at] * v_ref[m, here, at] - b_ref[s, here, at] * w_ref[m, here, at]
                    total = term if total is None else total + term
                sum_ref[chip ^ j, here, at] = total
        return carry

    lax.fori_loop(0, rows // step, tile, 0)
    out_ref[...] = sum_ref[...].astype(jnp.bfloat16)


def convolve(chips, inter, pieces):
    count, rows, width = inter[0].shape
    block = lambda n: pltpu.VMEM((n, rows, width), jnp.float32)
    return pl.pallas_call(
        functools.partial(conv_kernel, chips),
        out_shape=pltpu.VMEM((chips, rows, width), jnp.bfloat16),
        in_specs=[WHOLE] * (2 + 2 * chips),
        out_specs=WHOLE,
        scratch_shapes=[block(count + 1), block(count + 1), block(chips)],
        compiler_params=pltpu.CompilerParams(vmem_limit_bytes=16 << 20),
        cost_estimate=pl.CostEstimate(flops=count * count * rows * width * 4, bytes_accessed=0, transcendentals=0),
    )(*in_vmem(*inter, *pieces))


def dot(a, b):
    return jnp.dot(a, b, preferred_element_type=jnp.float32)


def packed(x):
    half = x.shape[0] // 2
    return jnp.concatenate([x[:half], x[half:]], axis=1)


def unpacked(x):
    size = x.shape[1] // 2
    return jnp.concatenate([x[:, :size], x[:, size:]], axis=0)


def moved(link_ref, turned_ref, x):
    return dot(dot(link_ref[...], x).astype(jnp.bfloat16), turned_ref[...])


def gather_kernel(*refs):
    chip = lax.axis_index(ENERGY) // 2
    *pieces, re_ref, im_ref, all_ref = refs
    for j, ref in zip(in_order(len(pieces)), pieces):
        all_ref[chip ^ j] = ref[...]
    chips, rows, width = all_ref.shape
    whole = all_ref[...].reshape(chips * rows, width)
    re_ref[...] = packed(whole[:, : width // 2])
    im_ref[...] = packed(whole[:, width // 2 :])


def gathered(pieces):
    chips, (rows, width) = len(pieces), pieces[0].shape
    part = ((chips * rows // 2, width), jnp.bfloat16)
    return call(gather_kernel, [part, part], pieces, [pltpu.VMEM((chips, rows, width), jnp.bfloat16)])


def adjoint(stack, sign):
    size = stack.shape[1]
    re, im = stack[:size], stack[size:]
    return jnp.concatenate([re, -im] if sign > 0 else [im, re], axis=0).T


def prepare_kernel(pair, link_ref, before_ref, green_ref, turned_ref, step_ref, turned_step_ref, *refs):
    stack_ref, first_ref, second_ref, far_stack_ref, far_first_ref, far_second_ref, half_a_ref, half_b_ref = refs
    slab = lax.axis_index(SLAB)
    turned_ref[...] = link_ref[...].T

    @pl.when(slab % 2 == 0)
    def _():
        step_ref[...] = link_ref[...]

    @pl.when(slab % 2 == 1)
    def _():
        step_ref[...] = dot(link_ref[...], before_ref[...]).astype(jnp.bfloat16)

    turned_step_ref[...] = step_ref[...].T
    size = green_ref.shape[0]
    stack_ref[:size] = green_ref[:, :size]
    stack_ref[size:] = green_ref[:, size:]
    first_ref[...] = adjoint(stack_ref[...], 1)
    second_ref[...] = adjoint(stack_ref[...], -1)

    @pl.when(slab // 2 == pair)
    def _():
        far_stack_ref[...] = dot(stack_ref[...], step_ref[...]).astype(jnp.bfloat16)
        far_first_ref[...] = adjoint(far_stack_ref[...], 1)
        far_second_ref[...] = adjoint(far_stack_ref[...], -1)
        quarter = size // 4
        columns = [far_stack_ref[:, i * quarter : (i + 1) * quarter] for i in range(4)]
        half_a_ref[...] = jnp.concatenate([columns[0], columns[2]], axis=1)
        half_b_ref[...] = jnp.concatenate([columns[1], columns[3]], axis=1)


def joined(refs):
    return jnp.concatenate([ref[...] for ref in refs], axis=0)


def carry_in(turn, link_ref, turned_ref, state, came, out_refs):
    rows = out_refs[0].shape[0]

    @pl.when(turn)
    def _():
        out = (unpacked(state).astype(jnp.float32) + moved(link_ref, turned_ref, unpacked(came))).astype(jnp.bfloat16)
        out = packed(out)
        for i, ref in enumerate(out_refs):
            ref[...] = out[i * rows : (i + 1) * rows]

    @pl.when(jnp.logical_not(turn))
    def _():
        for i, ref in enumerate(out_refs):
            ref[...] = state[i * rows : (i + 1) * rows]


def assembled(pieces, lanes, rows_ref):
    chip = lax.axis_index(ENERGY) // 2
    for j, ref in zip(in_order(len(pieces)), pieces):
        rows_ref[chip ^ j] = ref[:, lanes]
    chips, rows, size = rows_ref.shape
    return rows_ref[...].reshape(chips * rows, size)


def first_kernel(last_pair, part, link_ref, turned_ref, own_ref, *refs):
    *pieces, out_a_ref, out_b_ref, rows_ref = refs
    size = link_ref.shape[0]
    slab = lax.axis_index(SLAB)
    turn = jnp.logical_and(slab % 2 == 1, slab // 2 < last_pair)
    half = out_a_ref.shape[0]

    @pl.when(turn)
    def _():
        came = assembled(pieces, slice(part * size, (part + 1) * size), rows_ref)
        own = unpacked(own_ref[...]).astype(jnp.float32)
        out = packed((own + moved(link_ref, turned_ref, came)).astype(jnp.bfloat16))
        out_a_ref[...] = out[:half]
        out_b_ref[...] = out[half:]

    @pl.when(jnp.logical_not(turn))
    def _():
        out_a_ref[...] = own_ref[:half]
        out_b_ref[...] = own_ref[half:]


def arrived(refs):
    near, far = refs[: len(refs) // 2], refs[len(refs) // 2 :]
    return jnp.where(lax.axis_index(SLAB) % 2 == 0, joined(near), joined(far))


def advance_kernel(pair, link_ref, turned_ref, *refs):
    parts = len(refs) // 4
    state, came, outs = refs[:parts], refs[parts : 3 * parts], refs[3 * parts :]
    carry_in(lax.axis_index(SLAB) // 2 == pair, link_ref, turned_ref, joined(state), arrived(came), outs)


def base_kernel(last_pair, link_ref, turned_ref, stack_ref, first_ref, second_ref, *refs):
    *given, out_ref, re_ref, im_ref, rows_ref = refs
    state, pieces = given[:4], given[4:]
    size = link_ref.shape[0]
    slab = lax.axis_index(SLAB)
    turn = jnp.logical_and(slab % 2 == 1, slab // 2 == last_pair)
    for parts, part, ref in ((state[:2], 0, re_ref), (state[2:], 1, im_ref)):
        own = unpacked(joined(parts))

        @pl.when(turn)
        def _():
            came = assembled(pieces, slice(part * size, (part + 1) * size), rows_ref)
            ref[...] = (own.astype(jnp.float32) + moved(link_ref, turned_ref, came)).astype(jnp.bfloat16)

        @pl.when(jnp.logical_not(turn))
        def _():
            ref[...] = own

    re, im = dot(stack_ref[...], re_ref[...]), dot(stack_ref[...], im_ref[...])
    size = re.shape[1]
    left_re = (re[:size] - im[size:]).astype(jnp.bfloat16)
    left_im = (im[:size] + re[size:]).astype(jnp.bfloat16)
    out_ref[...] = dot(left_re, first_ref[...]) + dot(left_im, second_ref[...])


def left_kernel(pair, matrix_ref, *refs):
    *came, out_ref = refs

    @pl.when(lax.axis_index(SLAB) // 2 == pair)
    def _():
        out_ref[...] = dot(matrix_ref[...], unpacked(arrived(came)))


def late_kernel(pair, far_first_ref, far_second_ref, half_ref, base_ref, re_ref, im_ref, *refs):
    *came, out_ref, left_re_ref, left_im_ref, result_ref, sems = refs
    size, width = result_ref.shape
    turn = lax.axis_index(SLAB) // 2 == pair
    cut = width // 256 * 256 if width > 256 else width // 2

    @pl.when(turn)
    def _():
        im = im_ref[...] + dot(half_ref[...], unpacked(arrived(came)))
        left_re_ref[...] = (re_ref[:size] - im[size:]).astype(jnp.bfloat16)
        left_im_ref[...] = (im[:size] + re_ref[size:]).astype(jnp.bfloat16)

    copies = []
    for n, block in enumerate((slice(0, cut), slice(cut, width))):

        @pl.when(turn)
        def _():
            late = dot(left_re_ref[...], far_first_ref[:, block]) + dot(left_im_ref[...], far_second_ref[:, block])
            result_ref[:, block] = (base_ref[:, block] + late).astype(jnp.bfloat16)

        @pl.when(jnp.logical_not(turn))
        def _():
            result_ref[:, block] = base_ref[:, block].astype(jnp.bfloat16)

        copy = pltpu.make_async_copy(result_ref.at[:, block], out_ref.at[:, block], sems.at[n])
        copy.start()
        copies.append(copy)
    for copy in copies:
        copy.wait()


def local(g_lesser, g_retarded, screened, coupling):
    devices = lax.axis_size(ENERGY)
    slabs = lax.axis_size(SLAB)
    chips = devices // 2
    me = lax.axis_index(ENERGY)
    chip, side = me // 2, me % 2

    lesser = g_lesser[0, 0]
    size, width = lesser.shape
    rows = size // chips
    inter = screened[:, 0]
    inter_other = swap_with(inter, 1)
    spread = call(spread_kernel, [((devices, rows, width), jnp.float32)] * 2, [inter, inter_other])

    mine = [lax.dynamic_slice(lesser, (rows * (chip ^ j), 0), (rows, width)) for j in range(chips)]
    pieces = [mine[0]] + [swap_with(mine[j], 2 * j) for j in range(1, chips)]

    link = coupling[0]
    other_in_pair = {s: s ^ 1 for s in range(slabs)}
    link, spread = lax.optimization_barrier((link, spread))
    link_before = swap_slabs(link, other_in_pair)

    pieces = pieces + [swap_with(x, 1) for x in pieces]
    sigma = convolve(chips, spread, pieces)
    sigma, link_before = lax.optimization_barrier((sigma, link_before))
    own = [sigma[0]] + [swap_with(sigma[j], 2 * j) for j in in_order(chips)[1:]]
    came = [swap_slabs(x, other_in_pair) for x in own]
    own_re, own_im = gathered(own)

    own_re, own_im, link_before = lax.optimization_barrier((own_re, own_im, link_before))
    square = (link.shape, jnp.bfloat16)
    tall, wide = ((2 * size, size), jnp.bfloat16), ((size, 2 * size), jnp.bfloat16)
    thin = ((2 * size, size // 2), jnp.bfloat16)
    last_pair = slabs // 2 - 1
    prepared = call(
        functools.partial(prepare_kernel, last_pair),
        [square, square, square, tall, wide, wide, tall, wide, wide, thin, thin],
        [link, link_before, g_retarded[0, 0]],
    )
    turned, step, turned_step, *base, far_stack, far_first, far_second, half_a, half_b = prepared
    halves = [((size // 4, width), own_im.dtype)] * 2
    total = [((size, width), jnp.float32)]
    block = pltpu.VMEM((chips, rows, size), jnp.bfloat16)
    re = call(functools.partial(first_kernel, last_pair, 0), halves, [link, turned, own_re, *came], [block])
    im = call(functools.partial(first_kernel, last_pair, 1), halves, [link, turned, own_im, *came], [block])

    for s in range(1, slabs - 1, 2):
        pair = (s + 1) // 2
        near, far = {s: s + 1, s + 1: s}, {s + 1: s + 2, s + 2: s + 1}
        near_re = [swap_slabs(x, near, 2) for x in re]
        near_im = [swap_slabs(x, near, 2) for x in im]
        if pair == last_pair:
            near_im[1], came = lax.optimization_barrier((near_im[1], came))
        far_re = [swap_slabs(x, far) for x in near_re]
        far_im = [swap_slabs(x, far) for x in near_im]
        if pair < last_pair:
            advance = functools.partial(advance_kernel, pair)
            re = call(advance, halves, [step, turned_step, *re, *near_re, *far_re])
            im = call(advance, halves, [step, turned_step, *im, *near_im, *far_im])
    total = [((size, width), jnp.float32)]
    given = [link, turned, *base, *re, *im, *came]
    scratch = [pltpu.VMEM(link.shape, link.dtype)] * 2 + [block]
    (out,) = call(functools.partial(base_kernel, last_pair), total, given, scratch)
    left = functools.partial(left_kernel, last_pair)
    products = [((2 * size, size), jnp.float32)]
    far_re[0], out = lax.optimization_barrier((far_re[0], out))
    (left_re,) = call(left, products, [far_stack, *near_re, *far_re])
    far_im[0], left_re = lax.optimization_barrier((far_im[0], left_re))
    (left_im,) = call(left, products, [half_a, near_im[0], far_im[0]])
    given = [far_first, far_second, half_b, out, left_re, left_im, near_im[1], far_im[1]]
    out = pl.pallas_call(
        functools.partial(late_kernel, last_pair),
        out_shape=jax.ShapeDtypeStruct((size, width), jnp.bfloat16),
        in_specs=[WHOLE] * len(given),
        out_specs=pl.BlockSpec(memory_space=pl.ANY),
        scratch_shapes=[
            pltpu.VMEM((size, size), jnp.bfloat16),
            pltpu.VMEM((size, size), jnp.bfloat16),
            pltpu.VMEM((size, width), jnp.bfloat16),
            pltpu.SemaphoreType.DMA((2,)),
        ],
        compiler_params=pltpu.CompilerParams(vmem_limit_bytes=10 << 20),
    )(*in_vmem(*given))
    return out[None, None]


def solution(mesh):
    placed = (
        P(ENERGY, SLAB, None, None),
        P(ENERGY, SLAB, None, None),
        P(None, SLAB, ENERGY, None),
        P(SLAB, None, None),
    )
    return jax.shard_map(
        local,
        mesh=mesh,
        in_specs=placed,
        out_specs=P(ENERGY, SLAB, None, None),
        check_vma=False,
    )
```

```python
import functools

import jax
import jax.numpy as jnp
from jax import lax
from jax.experimental import pallas as pl
from jax.experimental.pallas import tpu as pltpu
from jax.sharding import PartitionSpec as P

ENERGY = "energy"
SLAB = "slab"
WHOLE = pl.BlockSpec(memory_space=pltpu.VMEM)


def in_vmem(*arrays):
    return [pltpu.with_memory_space_constraint(x, pltpu.VMEM) for x in arrays]


def in_order(chips):
    return [0] + sorted(range(1, chips), key=lambda j: (j & (j - 1) != 0, -j))


def swap_with(array, mask):
    devices = lax.axis_size(ENERGY)
    return lax.ppermute(array, ENERGY, [(i, i ^ mask) for i in range(devices)])


def swap_slabs(array, slab_to, idle=1):
    devices, slabs = lax.axis_size(ENERGY), lax.axis_size(SLAB)
    pairs = []
    for e in range(devices):
        for s in range(slabs):
            to = (e, slab_to[s]) if s in slab_to else (e ^ idle, s)
            pairs.append((e * slabs + s, to[0] * slabs + to[1]))
    return lax.ppermute(array, (ENERGY, SLAB), pairs)


def call(kernel, outs, given, scratch=()):
    outs = [pltpu.VMEM(shape, dtype) for shape, dtype in outs]
    return pl.pallas_call(
        kernel,
        out_shape=outs,
        in_specs=[WHOLE] * len(given),
        out_specs=[WHOLE] * len(outs),
        scratch_shapes=list(scratch),
        compiler_params=pltpu.CompilerParams(vmem_limit_bytes=10 << 20),
    )(*in_vmem(*given))


def spread_kernel(inter_ref, other_ref, w_ref, v_ref):
    side = lax.axis_index(ENERGY) % 2
    count, rows, width = inter_ref.shape
    left = lax.broadcasted_iota(jnp.int32, (2 * rows, width), 1) < width // 2
    for m in range(count):
        own, other = inter_ref[m].astype(jnp.float32), other_ref[m].astype(jnp.float32)
        x = jnp.concatenate([jnp.where(side == 0, own, other), jnp.where(side == 0, other, own)], axis=0)
        y = jnp.concatenate([x[:, width // 2 :], x[:, : width // 2]], axis=1)
        w_ref[m] = x
        v_ref[m] = jnp.where(left, -y, y)


def conv_kernel(chips, w_ref, v_ref, *refs):
    pieces = refs[: 2 * chips]
    out_ref, a_ref, b_ref, sum_ref = refs[2 * chips :]
    me = lax.axis_index(ENERGY)
    chip, side = me // 2, me % 2
    rows, width = w_ref.shape[1:]
    half = width // 2
    left = lax.broadcasted_iota(jnp.int32, (rows, width), 1) < half

    def swapped(x):
        return jnp.concatenate([x[:, half:], x[:, :half]], axis=1)

    @pl.when(side == 0)
    def _():
        a_ref[0] = jnp.zeros((rows, width), jnp.float32)
        b_ref[0] = jnp.zeros((rows, width), jnp.float32)

    for other in range(2):
        for j in range(chips):
            x = pieces[other * chips + j][...].astype(jnp.float32)
            y = swapped(x)
            slot = 2 * (chip ^ j) + (side ^ other) + 1 - side
            a_ref[slot] = jnp.where(left, x, y)
            b_ref[slot] = jnp.where(left, y, x)
    step = 8 if rows % 8 == 0 else rows
    lanes = 128 if width % 128 == 0 else width

    def tile(t, carry):
        here = pl.ds(pl.multiple_of(t * step, step), step)
        for c in range(0, width, lanes):
            at = pl.ds(c, lanes)
            for j in range(chips):
                total = None
                for m in range(2 * j + 2):
                    s = 2 * j + 1 - m
                    term = a_ref[s, here, at] * v_ref[m, here, at] - b_ref[s, here, at] * w_ref[m, here, at]
                    total = term if total is None else total + term
                sum_ref[chip ^ j, here, at] = total
        return carry

    lax.fori_loop(0, rows // step, tile, 0)
    out_ref[...] = sum_ref[...].astype(jnp.bfloat16)


def convolve(chips, inter, pieces):
    count, rows, width = inter[0].shape
    block = lambda n: pltpu.VMEM((n, rows, width), jnp.float32)
    return pl.pallas_call(
        functools.partial(conv_kernel, chips),
        out_shape=pltpu.VMEM((chips, rows, width), jnp.bfloat16),
        in_specs=[WHOLE] * (2 + 2 * chips),
        out_specs=WHOLE,
        scratch_shapes=[block(count + 1), block(count + 1), block(chips)],
        compiler_params=pltpu.CompilerParams(vmem_limit_bytes=16 << 20),
        cost_estimate=pl.CostEstimate(flops=count * count * rows * width * 4, bytes_accessed=0, transcendentals=0),
    )(*in_vmem(*inter, *pieces))


def dot(a, b):
    return jnp.dot(a, b, preferred_element_type=jnp.float32)


def packed(x):
    half = x.shape[0] // 2
    return jnp.concatenate([x[:half], x[half:]], axis=1)


def unpacked(x):
    size = x.shape[1] // 2
    return jnp.concatenate([x[:, :size], x[:, size:]], axis=0)


def moved(link_ref, turned_ref, x):
    return dot(dot(link_ref[...], x).astype(jnp.bfloat16), turned_ref[...])


def gather_kernel(*refs):
    chip = lax.axis_index(ENERGY) // 2
    *pieces, re_ref, im_ref, all_ref = refs
    for j, ref in zip(in_order(len(pieces)), pieces):
        all_ref[chip ^ j] = ref[...]
    chips, rows, width = all_ref.shape
    whole = all_ref[...].reshape(chips * rows, width)
    re_ref[...] = packed(whole[:, : width // 2])
    im_ref[...] = packed(whole[:, width // 2 :])


def gathered(pieces):
    chips, (rows, width) = len(pieces), pieces[0].shape
    part = ((chips * rows // 2, width), jnp.bfloat16)
    return call(gather_kernel, [part, part], pieces, [pltpu.VMEM((chips, rows, width), jnp.bfloat16)])


def adjoint(stack, sign):
    size = stack.shape[1]
    re, im = stack[:size], stack[size:]
    return jnp.concatenate([re, -im] if sign > 0 else [im, re], axis=0).T


def prepare_kernel(pair, link_ref, before_ref, green_ref, turned_ref, step_ref, turned_step_ref, *refs):
    stack_ref, first_ref, second_ref, far_stack_ref, far_first_ref, far_second_ref, half_a_ref, half_b_ref = refs
    slab = lax.axis_index(SLAB)
    turned_ref[...] = link_ref[...].T

    @pl.when(slab % 2 == 0)
    def _():
        step_ref[...] = link_ref[...]

    @pl.when(slab % 2 == 1)
    def _():
        step_ref[...] = dot(link_ref[...], before_ref[...]).astype(jnp.bfloat16)

    turned_step_ref[...] = step_ref[...].T
    size = green_ref.shape[0]
    stack_ref[:size] = green_ref[:, :size]
    stack_ref[size:] = green_ref[:, size:]
    first_ref[...] = adjoint(stack_ref[...], 1)
    second_ref[...] = adjoint(stack_ref[...], -1)

    @pl.when(slab // 2 == pair)
    def _():
        far_stack_ref[...] = dot(stack_ref[...], step_ref[...]).astype(jnp.bfloat16)
        far_first_ref[...] = adjoint(far_stack_ref[...], 1)
        far_second_ref[...] = adjoint(far_stack_ref[...], -1)
        quarter = size // 4
        columns = [far_stack_ref[:, i * quarter : (i + 1) * quarter] for i in range(4)]
        half_a_ref[...] = jnp.concatenate([columns[0], columns[2]], axis=1)
        half_b_ref[...] = jnp.concatenate([columns[1], columns[3]], axis=1)


def joined(refs):
    return jnp.concatenate([ref[...] for ref in refs], axis=0)


def carry_in(turn, link_ref, turned_ref, state, came, out_refs):
    rows = out_refs[0].shape[0]

    @pl.when(turn)
    def _():
        out = (unpacked(state).astype(jnp.float32) + moved(link_ref, turned_ref, unpacked(came))).astype(jnp.bfloat16)
        out = packed(out)
        for i, ref in enumerate(out_refs):
            ref[...] = out[i * rows : (i + 1) * rows]

    @pl.when(jnp.logical_not(turn))
    def _():
        for i, ref in enumerate(out_refs):
            ref[...] = state[i * rows : (i + 1) * rows]


def assembled(pieces, lanes, rows_ref):
    chip = lax.axis_index(ENERGY) // 2
    for j, ref in zip(in_order(len(pieces)), pieces):
        rows_ref[chip ^ j] = ref[:, lanes]
    chips, rows, size = rows_ref.shape
    return rows_ref[...].reshape(chips * rows, size)


def first_kernel(last_pair, part, link_ref, turned_ref, own_ref, *refs):
    *pieces, out_a_ref, out_b_ref, rows_ref = refs
    size = link_ref.shape[0]
    slab = lax.axis_index(SLAB)
    turn = jnp.logical_and(slab % 2 == 1, slab // 2 < last_pair)
    half = out_a_ref.shape[0]

    @pl.when(turn)
    def _():
        came = assembled(pieces, slice(part * size, (part + 1) * size), rows_ref)
        own = unpacked(own_ref[...]).astype(jnp.float32)
        out = packed((own + moved(link_ref, turned_ref, came)).astype(jnp.bfloat16))
        out_a_ref[...] = out[:half]
        out_b_ref[...] = out[half:]

    @pl.when(jnp.logical_not(turn))
    def _():
        out_a_ref[...] = own_ref[:half]
        out_b_ref[...] = own_ref[half:]


def arrived(refs):
    near, far = refs[: len(refs) // 2], refs[len(refs) // 2 :]
    return jnp.where(lax.axis_index(SLAB) % 2 == 0, joined(near), joined(far))


def advance_kernel(pair, link_ref, turned_ref, *refs):
    parts = len(refs) // 4
    state, came, outs = refs[:parts], refs[parts : 3 * parts], refs[3 * parts :]
    carry_in(lax.axis_index(SLAB) // 2 == pair, link_ref, turned_ref, joined(state), arrived(came), outs)


def base_kernel(last_pair, link_ref, turned_ref, stack_ref, first_ref, second_ref, *refs):
    *given, out_ref, re_ref, im_ref, rows_ref = refs
    state, pieces = given[:4], given[4:]
    size = link_ref.shape[0]
    slab = lax.axis_index(SLAB)
    turn = jnp.logical_and(slab % 2 == 1, slab // 2 == last_pair)
    for parts, part, ref in ((state[:2], 0, re_ref), (state[2:], 1, im_ref)):
        own = unpacked(joined(parts))

        @pl.when(turn)
        def _():
            came = assembled(pieces, slice(part * size, (part + 1) * size), rows_ref)
            ref[...] = (own.astype(jnp.float32) + moved(link_ref, turned_ref, came)).astype(jnp.bfloat16)

        @pl.when(jnp.logical_not(turn))
        def _():
            ref[...] = own

    re, im = dot(stack_ref[...], re_ref[...]), dot(stack_ref[...], im_ref[...])
    size = re.shape[1]
    left_re = (re[:size] - im[size:]).astype(jnp.bfloat16)
    left_im = (im[:size] + re[size:]).astype(jnp.bfloat16)
    out_ref[...] = dot(left_re, first_ref[...]) + dot(left_im, second_ref[...])


def left_kernel(pair, matrix_ref, *refs):
    *came, out_ref = refs

    @pl.when(lax.axis_index(SLAB) // 2 == pair)
    def _():
        out_ref[...] = dot(matrix_ref[...], unpacked(arrived(came)))


def late_kernel(pair, far_first_ref, far_second_ref, half_ref, base_ref, re_ref, im_ref, *refs):
    *came, out_ref, left_re_ref, left_im_ref, result_ref, sems = refs
    size, width = result_ref.shape
    turn = lax.axis_index(SLAB) // 2 == pair
    cut = width // 256 * 256 if width > 256 else width // 2

    @pl.when(turn)
    def _():
        im = im_ref[...] + dot(half_ref[...], unpacked(arrived(came)))
        left_re_ref[...] = (re_ref[:size] - im[size:]).astype(jnp.bfloat16)
        left_im_ref[...] = (im[:size] + re_ref[size:]).astype(jnp.bfloat16)

    copies = []
    for n, block in enumerate((slice(0, cut), slice(cut, width))):

        @pl.when(turn)
        def _():
            late = dot(left_re_ref[...], far_first_ref[:, block]) + dot(left_im_ref[...], far_second_ref[:, block])
            result_ref[:, block] = (base_ref[:, block] + late).astype(jnp.bfloat16)

        @pl.when(jnp.logical_not(turn))
        def _():
            result_ref[:, block] = base_ref[:, block].astype(jnp.bfloat16)

        copy = pltpu.make_async_copy(result_ref.at[:, block], out_ref.at[:, block], sems.at[n])
        copy.start()
        copies.append(copy)
    for copy in copies:
        copy.wait()


def local(g_lesser, g_retarded, screened, coupling):
    devices = lax.axis_size(ENERGY)
    slabs = lax.axis_size(SLAB)
    chips = devices // 2
    me = lax.axis_index(ENERGY)
    chip, side = me // 2, me % 2

    lesser = g_lesser[0, 0]
    size, width = lesser.shape
    rows = size // chips
    inter = screened[:, 0]
    inter_other = swap_with(inter, 1)
    spread = call(spread_kernel, [((devices, rows, width), jnp.float32)] * 2, [inter, inter_other])

    mine = [lax.dynamic_slice(lesser, (rows * (chip ^ j), 0), (rows, width)) for j in range(chips)]
    pieces = [mine[0]] + [swap_with(mine[j], 2 * j) for j in range(1, chips)]

    link = coupling[0]
    other_in_pair = {s: s ^ 1 for s in range(slabs)}
    pieces[1], link, spread = lax.optimization_barrier((pieces[1], link, spread))
    link_before = swap_slabs(link, other_in_pair)

    pieces = pieces + [swap_with(x, 1) for x in pieces]
    sigma = convolve(chips, spread, pieces)
    sigma, link_before = lax.optimization_barrier((sigma, link_before))
    own = [sigma[0]] + [swap_with(sigma[j], 2 * j) for j in in_order(chips)[1:]]
    came = [swap_slabs(x, other_in_pair) for x in own]
    own_re, own_im = gathered(own)

    own_re, own_im, link_before = lax.optimization_barrier((own_re, own_im, link_before))
    square = (link.shape, jnp.bfloat16)
    tall, wide = ((2 * size, size), jnp.bfloat16), ((size, 2 * size), jnp.bfloat16)
    thin = ((2 * size, size // 2), jnp.bfloat16)
    last_pair = slabs // 2 - 1
    prepared = call(
        functools.partial(prepare_kernel, last_pair),
        [square, square, square, tall, wide, wide, tall, wide, wide, thin, thin],
        [link, link_before, g_retarded[0, 0]],
    )
    turned, step, turned_step, *base, far_stack, far_first, far_second, half_a, half_b = prepared
    halves = [((size // 4, width), own_im.dtype)] * 2
    total = [((size, width), jnp.float32)]
    block = pltpu.VMEM((chips, rows, size), jnp.bfloat16)
    re = call(functools.partial(first_kernel, last_pair, 0), halves, [link, turned, own_re, *came], [block])
    im = call(functools.partial(first_kernel, last_pair, 1), halves, [link, turned, own_im, *came], [block])

    for s in range(1, slabs - 1, 2):
        pair = (s + 1) // 2
        near, far = {s: s + 1, s + 1: s}, {s + 1: s + 2, s + 2: s + 1}
        near_re = [swap_slabs(x, near, 2) for x in re]
        near_im = [swap_slabs(x, near, 4) for x in im]
        if pair == last_pair:
            near_im[1], came = lax.optimization_barrier((near_im[1], came))
        far_re = [swap_slabs(x, far) for x in near_re]
        far_im = [swap_slabs(x, far) for x in near_im]
        if pair < last_pair:
            advance = functools.partial(advance_kernel, pair)
            re = call(advance, halves, [step, turned_step, *re, *near_re, *far_re])
            im = call(advance, halves, [step, turned_step, *im, *near_im, *far_im])
    total = [((size, width), jnp.float32)]
    given = [link, turned, *base, *re, *im, *came]
    scratch = [pltpu.VMEM(link.shape, link.dtype)] * 2 + [block]
    (out,) = call(functools.partial(base_kernel, last_pair), total, given, scratch)
    left = functools.partial(left_kernel, last_pair)
    products = [((2 * size, size), jnp.float32)]
    far_re[0], out = lax.optimization_barrier((far_re[0], out))
    (left_re,) = call(left, products, [far_stack, *near_re, *far_re])
    far_im[0], left_re = lax.optimization_barrier((far_im[0], left_re))
    (left_im,) = call(left, products, [half_a, near_im[0], far_im[0]])
    given = [far_first, far_second, half_b, out, left_re, left_im, near_im[1], far_im[1]]
    out = pl.pallas_call(
        functools.partial(late_kernel, last_pair),
        out_shape=jax.ShapeDtypeStruct((size, width), jnp.bfloat16),
        in_specs=[WHOLE] * len(given),
        out_specs=pl.BlockSpec(memory_space=pl.ANY),
        scratch_shapes=[
            pltpu.VMEM((size, size), jnp.bfloat16),
            pltpu.VMEM((size, size), jnp.bfloat16),
            pltpu.VMEM((size, width), jnp.bfloat16),
            pltpu.SemaphoreType.DMA((2,)),
        ],
        compiler_params=pltpu.CompilerParams(vmem_limit_bytes=10 << 20),
    )(*in_vmem(*given))
    return out[None, None]


def solution(mesh):
    placed = (
        P(ENERGY, SLAB, None, None),
        P(ENERGY, SLAB, None, None),
        P(None, SLAB, ENERGY, None),
        P(SLAB, None, None),
    )
    return jax.shard_map(
        local,
        mesh=mesh,
        in_specs=placed,
        out_specs=P(ENERGY, SLAB, None, None),
        check_vma=False,
    )
```

```python
import functools

import jax
import jax.numpy as jnp
from jax import lax
from jax.experimental import pallas as pl
from jax.experimental.pallas import tpu as pltpu
from jax.sharding import PartitionSpec as P

ENERGY = "energy"
SLAB = "slab"
WHOLE = pl.BlockSpec(memory_space=pltpu.VMEM)


def in_vmem(*arrays):
    return [pltpu.with_memory_space_constraint(x, pltpu.VMEM) for x in arrays]


def swap_with(array, mask):
    devices = lax.axis_size(ENERGY)
    return lax.ppermute(array, ENERGY, [(i, i ^ mask) for i in range(devices)])


def swap_slabs(array, slab_to, idle=1):
    devices, slabs = lax.axis_size(ENERGY), lax.axis_size(SLAB)
    pairs = []
    for e in range(devices):
        for s in range(slabs):
            to = (e, slab_to[s]) if s in slab_to else (e ^ idle, s)
            pairs.append((e * slabs + s, to[0] * slabs + to[1]))
    return lax.ppermute(array, (ENERGY, SLAB), pairs)


def call(kernel, outs, given, scratch=()):
    outs = [pltpu.VMEM(shape, dtype) for shape, dtype in outs]
    return pl.pallas_call(
        kernel,
        out_shape=outs,
        in_specs=[WHOLE] * len(given),
        out_specs=[WHOLE] * len(outs),
        scratch_shapes=list(scratch),
        compiler_params=pltpu.CompilerParams(vmem_limit_bytes=10 << 20),
    )(*in_vmem(*given))


def spread_kernel(inter_ref, other_ref, w_ref, v_ref):
    side = lax.axis_index(ENERGY) % 2
    count, rows, width = inter_ref.shape
    left = lax.broadcasted_iota(jnp.int32, (2 * rows, width), 1) < width // 2
    for m in range(count):
        own, other = inter_ref[m].astype(jnp.float32), other_ref[m].astype(jnp.float32)
        x = jnp.concatenate([jnp.where(side == 0, own, other), jnp.where(side == 0, other, own)], axis=0)
        y = jnp.concatenate([x[:, width // 2 :], x[:, : width // 2]], axis=1)
        w_ref[m] = x
        v_ref[m] = jnp.where(left, -y, y)


def conv_kernel(chips, w_ref, v_ref, *refs):
    pieces = refs[: 2 * chips]
    out_ref, a_ref, b_ref, sum_ref = refs[2 * chips :]
    me = lax.axis_index(ENERGY)
    chip, side = me // 2, me % 2
    rows, width = w_ref.shape[1:]
    half = width // 2
    left = lax.broadcasted_iota(jnp.int32, (rows, width), 1) < half

    def swapped(x):
        return jnp.concatenate([x[:, half:], x[:, :half]], axis=1)

    @pl.when(side == 0)
    def _():
        a_ref[0] = jnp.zeros((rows, width), jnp.float32)
        b_ref[0] = jnp.zeros((rows, width), jnp.float32)

    for other in range(2):
        for j in range(chips):
            x = pieces[other * chips + j][...].astype(jnp.float32)
            y = swapped(x)
            slot = 2 * (chip ^ j) + (side ^ other) + 1 - side
            a_ref[slot] = jnp.where(left, x, y)
            b_ref[slot] = jnp.where(left, y, x)
    step = 8 if rows % 8 == 0 else rows
    lanes = 128 if width % 128 == 0 else width

    def tile(t, carry):
        here = pl.ds(pl.multiple_of(t * step, step), step)
        for c in range(0, width, lanes):
            at = pl.ds(c, lanes)
            for j in range(chips):
                total = None
                for m in range(2 * j + 2):
                    s = 2 * j + 1 - m
                    term = a_ref[s, here, at] * v_ref[m, here, at] - b_ref[s, here, at] * w_ref[m, here, at]
                    total = term if total is None else total + term
                sum_ref[chip ^ j, here, at] = total
        return carry

    lax.fori_loop(0, rows // step, tile, 0)
    out_ref[...] = sum_ref[...].astype(jnp.bfloat16)


def convolve(chips, inter, pieces):
    count, rows, width = inter[0].shape
    block = lambda n: pltpu.VMEM((n, rows, width), jnp.float32)
    return pl.pallas_call(
        functools.partial(conv_kernel, chips),
        out_shape=pltpu.VMEM((chips, rows, width), jnp.bfloat16),
        in_specs=[WHOLE] * (2 + 2 * chips),
        out_specs=WHOLE,
        scratch_shapes=[block(count + 1), block(count + 1), block(chips)],
        compiler_params=pltpu.CompilerParams(vmem_limit_bytes=16 << 20),
        cost_estimate=pl.CostEstimate(flops=count * count * rows * width * 4, bytes_accessed=0, transcendentals=0),
    )(*in_vmem(*inter, *pieces))


def dot(a, b):
    return jnp.dot(a, b, preferred_element_type=jnp.float32)


def packed(x):
    half = x.shape[0] // 2
    return jnp.concatenate([x[:half], x[half:]], axis=1)


def unpacked(x):
    size = x.shape[1] // 2
    return jnp.concatenate([x[:, :size], x[:, size:]], axis=0)


def moved(link_ref, turned_ref, x):
    return dot(dot(link_ref[...], x).astype(jnp.bfloat16), turned_ref[...])


def gather_kernel(*refs):
    chip = lax.axis_index(ENERGY) // 2
    *pieces, re_ref, im_ref, all_ref = refs
    for j, ref in enumerate(pieces):
        all_ref[chip ^ j] = ref[...]
    chips, rows, width = all_ref.shape
    whole = all_ref[...].reshape(chips * rows, width)
    re_ref[...] = packed(whole[:, : width // 2])
    im_ref[...] = packed(whole[:, width // 2 :])


def gathered(pieces):
    chips, (rows, width) = len(pieces), pieces[0].shape
    part = ((chips * rows // 2, width), jnp.bfloat16)
    return call(gather_kernel, [part, part], pieces, [pltpu.VMEM((chips, rows, width), jnp.bfloat16)])


def adjoint(stack, sign):
    size = stack.shape[1]
    re, im = stack[:size], stack[size:]
    return jnp.concatenate([re, -im] if sign > 0 else [im, re], axis=0).T


def prepare_kernel(pair, link_ref, before_ref, green_ref, turned_ref, step_ref, turned_step_ref, *refs):
    stack_ref, first_ref, second_ref, far_stack_ref, far_first_ref, far_second_ref, half_a_ref, half_b_ref = refs
    slab = lax.axis_index(SLAB)
    turned_ref[...] = link_ref[...].T

    @pl.when(slab % 2 == 0)
    def _():
        step_ref[...] = link_ref[...]

    @pl.when(slab % 2 == 1)
    def _():
        step_ref[...] = dot(link_ref[...], before_ref[...]).astype(jnp.bfloat16)

    turned_step_ref[...] = step_ref[...].T
    size = green_ref.shape[0]
    stack_ref[:size] = green_ref[:, :size]
    stack_ref[size:] = green_ref[:, size:]
    first_ref[...] = adjoint(stack_ref[...], 1)
    second_ref[...] = adjoint(stack_ref[...], -1)

    @pl.when(slab // 2 == pair)
    def _():
        far_stack_ref[...] = dot(stack_ref[...], step_ref[...]).astype(jnp.bfloat16)
        far_first_ref[...] = adjoint(far_stack_ref[...], 1)
        far_second_ref[...] = adjoint(far_stack_ref[...], -1)
        quarter = size // 4
        columns = [far_stack_ref[:, i * quarter : (i + 1) * quarter] for i in range(4)]
        half_a_ref[...] = jnp.concatenate([columns[0], columns[2]], axis=1)
        half_b_ref[...] = jnp.concatenate([columns[1], columns[3]], axis=1)


def joined(refs):
    return jnp.concatenate([ref[...] for ref in refs], axis=0)


def carry_in(turn, link_ref, turned_ref, state, came, out_refs):
    rows = out_refs[0].shape[0]

    @pl.when(turn)
    def _():
        out = (unpacked(state).astype(jnp.float32) + moved(link_ref, turned_ref, unpacked(came))).astype(jnp.bfloat16)
        out = packed(out)
        for i, ref in enumerate(out_refs):
            ref[...] = out[i * rows : (i + 1) * rows]

    @pl.when(jnp.logical_not(turn))
    def _():
        for i, ref in enumerate(out_refs):
            ref[...] = state[i * rows : (i + 1) * rows]


def assembled(pieces, lanes, rows_ref):
    chip = lax.axis_index(ENERGY) // 2
    for j, ref in enumerate(pieces):
        rows_ref[chip ^ j] = ref[:, lanes]
    chips, rows, size = rows_ref.shape
    return rows_ref[...].reshape(chips * rows, size)


def first_kernel(last_pair, link_ref, turned_ref, own_re_ref, own_im_ref, *refs):
    *pieces, re_a_ref, re_b_ref, im_a_ref, im_b_ref, rows_ref = refs
    parts = ((own_re_ref, re_a_ref, re_b_ref), (own_im_ref, im_a_ref, im_b_ref))
    size = link_ref.shape[0]
    slab = lax.axis_index(SLAB)
    turn = jnp.logical_and(slab % 2 == 1, slab // 2 < last_pair)
    half = re_a_ref.shape[0]

    @pl.when(turn)
    def _():
        for part, (own_ref, out_a_ref, out_b_ref) in enumerate(parts):
            came = assembled(pieces, slice(part * size, (part + 1) * size), rows_ref)
            own = unpacked(own_ref[...]).astype(jnp.float32)
            out = packed((own + moved(link_ref, turned_ref, came)).astype(jnp.bfloat16))
            out_a_ref[...] = out[:half]
            out_b_ref[...] = out[half:]

    @pl.when(jnp.logical_not(turn))
    def _():
        for own_ref, out_a_ref, out_b_ref in parts:
            out_a_ref[...] = own_ref[:half]
            out_b_ref[...] = own_ref[half:]


def arrived(refs):
    near, far = refs[: len(refs) // 2], refs[len(refs) // 2 :]
    return jnp.where(lax.axis_index(SLAB) % 2 == 0, joined(near), joined(far))


def advance_kernel(pair, link_ref, turned_ref, *refs):
    parts = len(refs) // 4
    state, came, outs = refs[:parts], refs[parts : 3 * parts], refs[3 * parts :]
    carry_in(lax.axis_index(SLAB) // 2 == pair, link_ref, turned_ref, joined(state), arrived(came), outs)


def base_kernel(last_pair, link_ref, turned_ref, stack_ref, first_ref, second_ref, *refs):
    *given, out_ref, re_ref, im_ref, rows_ref = refs
    state, pieces = given[:4], given[4:]
    size = link_ref.shape[0]
    slab = lax.axis_index(SLAB)
    turn = jnp.logical_and(slab % 2 == 1, slab // 2 == last_pair)
    for parts, part, ref in ((state[:2], 0, re_ref), (state[2:], 1, im_ref)):
        own = unpacked(joined(parts))

        @pl.when(turn)
        def _():
            came = assembled(pieces, slice(part * size, (part + 1) * size), rows_ref)
            ref[...] = (own.astype(jnp.float32) + moved(link_ref, turned_ref, came)).astype(jnp.bfloat16)

        @pl.when(jnp.logical_not(turn))
        def _():
            ref[...] = own

    re, im = dot(stack_ref[...], re_ref[...]), dot(stack_ref[...], im_ref[...])
    size = re.shape[1]
    left_re = (re[:size] - im[size:]).astype(jnp.bfloat16)
    left_im = (im[:size] + re[size:]).astype(jnp.bfloat16)
    out_ref[...] = dot(left_re, first_ref[...]) + dot(left_im, second_ref[...])


def left_kernel(pair, matrix_ref, *refs):
    *came, out_ref = refs

    @pl.when(lax.axis_index(SLAB) // 2 == pair)
    def _():
        out_ref[...] = dot(matrix_ref[...], unpacked(arrived(came)))


def late_kernel(pair, far_first_ref, far_second_ref, half_ref, base_ref, re_ref, im_ref, *refs):
    *came, out_ref, left_re_ref, left_im_ref, result_ref, sems = refs
    size, width = result_ref.shape
    turn = lax.axis_index(SLAB) // 2 == pair
    cut = width // 256 * 256 if width > 256 else width // 2

    @pl.when(turn)
    def _():
        im = im_ref[...] + dot(half_ref[...], unpacked(arrived(came)))
        left_re_ref[...] = (re_ref[:size] - im[size:]).astype(jnp.bfloat16)
        left_im_ref[...] = (im[:size] + re_ref[size:]).astype(jnp.bfloat16)

    copies = []
    for n, block in enumerate((slice(0, cut), slice(cut, width))):

        @pl.when(turn)
        def _():
            late = dot(left_re_ref[...], far_first_ref[:, block]) + dot(left_im_ref[...], far_second_ref[:, block])
            result_ref[:, block] = (base_ref[:, block] + late).astype(jnp.bfloat16)

        @pl.when(jnp.logical_not(turn))
        def _():
            result_ref[:, block] = base_ref[:, block].astype(jnp.bfloat16)

        copy = pltpu.make_async_copy(result_ref.at[:, block], out_ref.at[:, block], sems.at[n])
        copy.start()
        copies.append(copy)
    for copy in copies:
        copy.wait()


def local(g_lesser, g_retarded, screened, coupling):
    devices = lax.axis_size(ENERGY)
    slabs = lax.axis_size(SLAB)
    chips = devices // 2
    me = lax.axis_index(ENERGY)
    chip, side = me // 2, me % 2

    lesser = g_lesser[0, 0]
    size, width = lesser.shape
    rows = size // chips
    inter = screened[:, 0]
    inter_other = swap_with(inter, 1)
    spread = call(spread_kernel, [((devices, rows, width), jnp.float32)] * 2, [inter, inter_other])

    mine = [lax.dynamic_slice(lesser, (rows * (chip ^ j), 0), (rows, width)) for j in range(chips)]
    pieces = [mine[0]] + [swap_with(mine[j], 2 * j) for j in range(1, chips)]

    link = coupling[0]
    other_in_pair = {s: s ^ 1 for s in range(slabs)}
    pieces[1], link, spread = lax.optimization_barrier((pieces[1], link, spread))
    link_before = swap_slabs(link, other_in_pair)

    pieces = pieces + [swap_with(x, 1) for x in pieces]
    sigma = convolve(chips, spread, pieces)
    sigma, link_before = lax.optimization_barrier((sigma, link_before))
    own = [sigma[0]] + [swap_with(sigma[j], 2 * j) for j in range(1, chips)]
    came = [swap_slabs(x, other_in_pair) for x in own]
    own_re, own_im = gathered(own)

    own_re, own_im, link_before = lax.optimization_barrier((own_re, own_im, link_before))
    square = (link.shape, jnp.bfloat16)
    tall, wide = ((2 * size, size), jnp.bfloat16), ((size, 2 * size), jnp.bfloat16)
    thin = ((2 * size, size // 2), jnp.bfloat16)
    last_pair = slabs // 2 - 1
    prepared = call(
        functools.partial(prepare_kernel, last_pair),
        [square, square, square, tall, wide, wide, tall, wide, wide, thin, thin],
        [link, link_before, g_retarded[0, 0]],
    )
    turned, step, turned_step, *base, far_stack, far_first, far_second, half_a, half_b = prepared
    halves = [((size // 4, width), own_im.dtype)] * 2
    total = [((size, width), jnp.float32)]
    block = pltpu.VMEM((chips, rows, size), jnp.bfloat16)
    given = [link, turned, own_re, own_im, *came]
    states = call(functools.partial(first_kernel, last_pair), halves * 2, given, [block])
    re, im = states[:2], states[2:]

    for s in range(1, slabs - 1, 2):
        pair = (s + 1) // 2
        near, far = {s: s + 1, s + 1: s}, {s + 1: s + 2, s + 2: s + 1}
        near_re = [swap_slabs(x, near, 2) for x in re]
        near_im = [swap_slabs(x, near, 4) for x in im]
        if pair == last_pair:
            near_im[1], came = lax.optimization_barrier((near_im[1], came))
        far_re = [swap_slabs(x, far) for x in near_re]
        far_im = [swap_slabs(x, far) for x in near_im]
        if pair < last_pair:
            advance = functools.partial(advance_kernel, pair)
            re = call(advance, halves, [step, turned_step, *re, *near_re, *far_re])
            im = call(advance, halves, [step, turned_step, *im, *near_im, *far_im])
    total = [((size, width), jnp.float32)]
    given = [link, turned, *base, *re, *im, *came]
    scratch = [pltpu.VMEM(link.shape, link.dtype)] * 2 + [block]
    (out,) = call(functools.partial(base_kernel, last_pair), total, given, scratch)
    left = functools.partial(left_kernel, last_pair)
    products = [((2 * size, size), jnp.float32)]
    far_re[0], out = lax.optimization_barrier((far_re[0], out))
    (left_re,) = call(left, products, [far_stack, *near_re, *far_re])
    far_im[0], left_re = lax.optimization_barrier((far_im[0], left_re))
    (left_im,) = call(left, products, [half_a, near_im[0], far_im[0]])
    given = [far_first, far_second, half_b, out, left_re, left_im, near_im[1], far_im[1]]
    out = pl.pallas_call(
        functools.partial(late_kernel, last_pair),
        out_shape=jax.ShapeDtypeStruct((size, width), jnp.bfloat16),
        in_specs=[WHOLE] * len(given),
        out_specs=pl.BlockSpec(memory_space=pl.ANY),
        scratch_shapes=[
            pltpu.VMEM((size, size), jnp.bfloat16),
            pltpu.VMEM((size, size), jnp.bfloat16),
            pltpu.VMEM((size, width), jnp.bfloat16),
            pltpu.SemaphoreType.DMA((2,)),
        ],
        compiler_params=pltpu.CompilerParams(vmem_limit_bytes=10 << 20),
    )(*in_vmem(*given))
    return out[None, None]


def solution(mesh):
    placed = (
        P(ENERGY, SLAB, None, None),
        P(ENERGY, SLAB, None, None),
        P(None, SLAB, ENERGY, None),
        P(SLAB, None, None),
    )
    return jax.shard_map(
        local,
        mesh=mesh,
        in_specs=placed,
        out_specs=P(ENERGY, SLAB, None, None),
        check_vma=False,
    )
```
